32 devices in a mesh: row: 2 (over x), col: 4 (over y, core), mem: 4 (over z).
Axes of the slice: x: 2, y: 2, z: 4, core: 2. Of those that a mesh axis runs over, the one named last changes fastest.
Arguments:
- adj_final: float32 [1024, 4096], P(('mem', 'row'), 'col'), parts along dimension 0, may hold values from -6 to 6
- kappa: float32 [1024, 4096], P(('mem', 'row'), 'col'), parts along dimension 0, may hold values from 0.1 to 1
- elev_early: float32 [1024, 4096], P(('mem', 'row'), 'col'), parts along dimension 0, may hold values from -6 to 6
- elev_late: float32 [1024, 4096], P(('mem', 'row'), 'col'), parts along dimension 0, may hold values from -6 to 6
- basis: bfloat16 [8, 4, 4, 1024, 256], P(('mem', 'row'), 'col'), parts along dimension 0, may hold values from -0.1875 to 0.1875
- basis_index: int32 [8, 4, 512], P(('mem', 'row'), 'col'), parts along dimension 0, may hold values from 0 to 3
- intersection_patch: int32 [8, 4, 512], P(('mem', 'row'), 'col'), parts along dimension 0, may hold values from 0 to 127, as said below
- owner_row: int32 [16, 128], P(('mem', 'col')), parts along dimension 0, may hold values from 0 to 127, as said below
Outputs:
- adj_start: float32 [1024, 4096], P(('mem', 'row'), 'col'), parts along dimension 0
- coeff_grad: float32 [16, 128, 256], P(('mem', 'col'), 'row'), parts along dimension 0
The draws below stay inside these ranges and needn't reach their ends.
There are 4 independent parts, one for each index of `mem`. The reference program is written for one: setup_inputs(seed, part) draws one part's arguments, and reference() takes and returns one part's arrays. A program takes and returns all parts, laid end to end along the dimension named above; each array names one. Nothing has to cross between parts.
Inputs may be any that keep to these rules, and one draw needn't show every extreme that they name: Each row of owner_row is a permutation of 0 to 127; the owner of patch p in strip j is owner_row[j, p] // 64. `intersection_patch`: of the 512 entries of one tile (i, j), at most 512 name patches of any one owner r (patches p with owner_row[j, p] // 64 = r), and exactly 512 name patches of some owner.
All inputs are finite; a program needn't handle non-finite values.
Results may differ from the reference program's by a relative error of at most 0.0029.
Values sent between devices are 32-bit elements; how exact they have to be, the bound alone decides.
A program may use at most 64 MiB of HBM per device.

```python
import math
import jax
import jax.numpy as jnp
from jax import lax

TR = 128
TC = 1024
BS = 32
NCOEF = 256
OV = 4
NQ = 4
PD = 64
NR = 256
NC = 4096
NB = 128
ENTRIES = 512
CAP = 512
PATCHES = 128
N_ROW = 2
N_COL = 4


def joint_lists(key):
    base = jax.random.fold_in(key, 7)
    perm_keys = jax.random.split(jax.random.fold_in(base, 1), N_COL)
    owner_table = jax.vmap(lambda k: jax.random.permutation(k, PATCHES))(perm_keys).astype(jnp.int32)
    inverse = jnp.argsort(owner_table, axis=1).astype(jnp.int32)
    slot_total = 2 * ENTRIES
    device_keys = jax.random.split(jax.random.fold_in(base, 2), N_ROW * N_COL)
    columns = jnp.arange(N_ROW * N_COL, dtype=jnp.int32) % N_COL

    def one_device(dkey, column):
        key_a, key_b, key_c, key_d = jax.random.split(dkey, 4)
        forced = jax.random.randint(key_a, (), 0, N_ROW).astype(jnp.int32)
        score = jax.random.randint(key_b, (slot_total,), 0, 1 << 14).astype(jnp.int32)
        owners = jnp.arange(slot_total, dtype=jnp.int32) // CAP
        ranking = jnp.where(owners == forced, 0, 1 << 28) + score * slot_total + jnp.arange(slot_total, dtype=jnp.int32)
        chosen = jnp.argsort(ranking)[:ENTRIES].astype(jnp.int32)
        shuffle = jax.random.permutation(key_c, ENTRIES).astype(jnp.int32)
        entry_owner = (chosen // CAP)[shuffle]
        within = jax.random.randint(key_d, (ENTRIES,), 0, PD).astype(jnp.int32)
        return inverse[column, entry_owner * PD + within]
    patches = jax.vmap(one_device)(device_keys, columns)
    return (owner_table, patches.reshape(N_ROW, N_COL, ENTRIES).astype(jnp.int32))


def draw_intersection_patch(key, part):
    return joint_lists(key)[1]


def draw_owner_row(key, part):
    return joint_lists(key)[0]


def with_ends(array, key, low, top_value):
    longest = array.shape.index(max(array.shape))
    spots = []
    for shift in (0, 1):
        where = [jax.random.randint(jax.random.fold_in(key, axis), (), 0, length) for axis, length in enumerate(array.shape)]
        where[longest] = (where[longest] + shift) % array.shape[longest]
        spots.append(tuple(where))
    return array.at[spots[0]].set(low).at[spots[1]].set(top_value)


def shard_levels(stream_key, shape, pieces, smallest, top_value):
    def one(axis_at, shards_of):
        steps = jax.random.uniform(jax.random.fold_in(jax.random.fold_in(stream_key, 6), axis_at), (shards_of,), jnp.float32, smallest / len(pieces), top_value / len(pieces))
        return jnp.repeat(jnp.exp(steps), shape[axis_at] // shards_of).reshape((-1,) + (1,) * (len(shape) - axis_at - 1))

    factor_of = one(*pieces[0])
    for cut in pieces[1:]:
        factor_of = factor_of * one(*cut)
    return factor_of


def gaussian(key, dims, spread, reach, pieces=(), kind=jnp.bfloat16):
    gain = shard_levels(key, dims, pieces, -0.22, 0.18) if pieces else 1.0
    result = jax.random.normal(key, dims, jnp.float32) * spread * gain
    return jnp.minimum(jnp.maximum(result, -reach), reach).astype(kind)


def setup_inputs(seed: int = 0, part: int = 0) -> dict:
    splits = jax.random.split(jax.random.key(seed), 9)
    part_splits = jax.random.split(jax.random.fold_in(splits[8], part), 9)
    adj_final = gaussian(part_splits[0], (NR, NC), 1.0, 6.0, ((0, 2), (1, 4)), jnp.float32)
    kappa = jnp.clip(jnp.exp(math.log(1.0) - 2.3025851 * jax.random.uniform(part_splits[1], (NR, NC), jnp.float32) ** shard_levels(part_splits[1], (NR, NC), ((0, 2), (1, 4)), -0.2, 0.2)), 0.1, 1.0)
    elev_early = gaussian(part_splits[2], (NR, NC), 1.0, 6.0, ((0, 2), (1, 4)), jnp.float32)
    elev_late = gaussian(part_splits[3], (NR, NC), 1.0, 6.0, ((0, 2), (1, 4)), jnp.float32)
    basis = gaussian(part_splits[4], (N_ROW, N_COL, NQ, BS * BS, NCOEF), (BS * BS) ** -0.5, 0.1875, ((0, 2), (1, 4)))
    basis_index = with_ends(jax.random.randint(part_splits[5], (N_ROW, N_COL, ENTRIES), 0, NQ), jax.random.fold_in(part_splits[5], 1), 0, NQ - 1).astype(jnp.int32)
    intersection_patch = draw_intersection_patch(jax.random.fold_in(jax.random.fold_in(splits[8], part), 71), part)
    owner_row = draw_owner_row(jax.random.fold_in(jax.random.fold_in(splits[8], part), 71), part)
    return dict(adj_final=adj_final, kappa=kappa, elev_early=elev_early, elev_late=elev_late, basis=basis, basis_index=basis_index, intersection_patch=intersection_patch, owner_row=owner_row)


DT = 0.2


def adjoint_step(adjoint, coef):
    padded = jnp.pad(adjoint, 1)
    centre = padded[1:-1, 1:-1]
    lap = padded[2:, 1:-1] + padded[:-2, 1:-1] + padded[1:-1, 2:] + padded[1:-1, :-2] - 4.0 * centre
    return adjoint + coef * lap


def reference(adj_final, kappa, elev_early, elev_late, basis, basis_index, intersection_patch, owner_row):
    coef_late = DT * kappa / (1.0 + elev_late * elev_late)
    coef_early = DT * kappa / (1.0 + elev_early * elev_early)
    adj_mid = adjoint_step(adj_final, coef_late)
    adj_start = adjoint_step(adj_mid, coef_early)
    grad_field = (DT * (adj_final + adj_mid)).astype(jnp.bfloat16)
    blocks = grad_field.reshape(N_ROW, TR // BS, BS, N_COL, TC // BS, BS)
    blocks = blocks.transpose(0, 3, 1, 4, 2, 5).reshape(N_ROW * N_COL, NB, BS * BS)
    tables = basis.reshape(N_ROW * N_COL, NQ, BS * BS, NCOEF)
    indices = basis_index.reshape(N_ROW * N_COL, ENTRIES).astype(jnp.int32)

    def one_tile(items):
        block_rows, table, index = items
        products = jnp.einsum('bk,qkn->qbn', block_rows.astype(jnp.float32), table.astype(jnp.float32))
        picked = products[index.reshape(NB, OV), jnp.arange(NB, dtype=jnp.int32)[:, None]]
        return picked.reshape(ENTRIES, NCOEF)

    contrib = lax.map(one_tile, (blocks, tables, indices))
    columns = jnp.arange(N_ROW * N_COL, dtype=jnp.int32) % N_COL
    patches = intersection_patch.reshape(N_ROW * N_COL, ENTRIES).astype(jnp.int32)
    targets = owner_row[columns[:, None], patches] + columns[:, None] * PATCHES
    coeff_grad = jax.ops.segment_sum(contrib.reshape(-1, NCOEF), targets.reshape(-1), num_segments=N_COL * PATCHES)
    return adj_start, coeff_grad.reshape(N_COL, PATCHES, NCOEF)
```

```python
import functools

import jax
import jax.numpy as jnp
from jax import lax
from jax.experimental import pallas as pl
from jax.experimental.pallas import tpu as pltpu
from jax.sharding import PartitionSpec as P

BS = 32
OV = 4
LANES = 128
DT = 0.2
MESH = pl.DeviceIdType.MESH


def kernel(
    n_row,
    n_col,
    adj_hbm,
    kappa_hbm,
    early_hbm,
    late_hbm,
    basis_hbm,
    index_ref,
    patch_ref,
    owner_ref,
    start_ref,
    grad_ref,
    adj,
    kappa,
    early,
    late,
    basis,
    mid,
    field,
    blocks,
    counts,
    row_out,
    row_in,
    col_out,
    col_in,
    part_out,
    part_in,
    load_sem,
    halo_send,
    halo_recv,
    part_send,
    part_recv,
):
    rows, cols = adj.shape
    tiles = cols // LANES
    group = LANES // BS
    high = rows // BS
    nblock = blocks.shape[0]
    nbasis, depth, ncoef = basis.shape
    owned = grad_ref.shape[0]
    i = lax.axis_index("row")
    j = lax.axis_index("col")
    sides = (
        (i > 0, {"row": i - 1}),
        (i < n_row - 1, {"row": i + 1}),
        (j > 0, {"col": j - 1}),
        (j < n_col - 1, {"col": j + 1}),
    )
    partners = [lax.rem(i + step, n_row) for step in range(1, n_row)]

    loads = [
        pltpu.make_async_copy(source, target, load_sem.at[n])
        for n, (source, target) in enumerate(
            ((adj_hbm, adj), (late_hbm, late), (kappa_hbm, kappa), (early_hbm, early), (basis_hbm, basis))
        )
    ]

    barrier = pltpu.get_barrier_semaphore()
    for partner in partners:
        pl.semaphore_signal(barrier, inc=1, device_id={"row": partner}, device_id_type=MESH)
    for exists, target in sides[2:]:

        @pl.when(exists)
        def _(target=target):
            pl.semaphore_signal(barrier, inc=1, device_id=target, device_id_type=MESH)

    for load in loads:
        load.start()

    def halo(step, side):
        out, into = (row_out, row_in) if side < 2 else (col_out, col_in)
        return pltpu.make_async_remote_copy(
            src_ref=out.at[step, side % 2],
            dst_ref=into.at[step, 1 - side % 2],
            send_sem=halo_send.at[step, side],
            recv_sem=halo_recv.at[step, side ^ 1],
            device_id=sides[side][1],
            device_id_type=MESH,
        )

    def halo_arrival(step, side):
        into = row_in if side < 2 else col_in
        out = row_out if side < 2 else col_out
        return pltpu.make_async_remote_copy(
            src_ref=out.at[step, side % 2],
            dst_ref=into.at[step, side % 2],
            send_sem=halo_send.at[step, side],
            recv_sem=halo_recv.at[step, side],
            device_id=sides[side][1],
            device_id_type=MESH,
        )

    def send_edges(step, ref):
        row_out[step, 0] = ref[0:1, :]
        row_out[step, 1] = ref[rows - 1 : rows, :]
        col_out[step, 0] = ref[:, 0:LANES].T[0:1, :]
        col_out[step, 1] = ref[:, cols - LANES : cols].T[LANES - 1 : LANES, :]
        for side in range(4):

            @pl.when(sides[side][0])
            def _(side=side):
                halo(step, side).start()

    def receive_edges(step):
        for side in range(4):
            into = row_in if side < 2 else col_in

            @pl.when(sides[side][0])
            def _(side=side):
                halo_arrival(step, side).wait_recv()

            @pl.when(jnp.logical_not(sides[side][0]))
            def _(side=side, into=into):
                into[step, side % 2] = jnp.zeros(into.shape[2:], jnp.float32)

    lane = lax.broadcasted_iota(jnp.int32, (rows, LANES), 1)
    line = lax.broadcasted_iota(jnp.int32, (rows, LANES), 0)

    def tile(ref, t):
        return ref[:, t * LANES : (t + 1) * LANES]

    def inner_step(ref, coef, t):
        centre = tile(ref, t)
        up = jnp.where(line == 0, 0.0, pltpu.roll(centre, 1, 0))
        down = jnp.where(line == rows - 1, 0.0, pltpu.roll(centre, rows - 1, 0))
        before = pltpu.roll(tile(ref, t - 1), 1, 1) if t else 0.0
        after = pltpu.roll(tile(ref, t + 1), LANES - 1, 1) if t < tiles - 1 else 0.0
        left = jnp.where(lane == 0, before, pltpu.roll(centre, 1, 1))
        right = jnp.where(lane == LANES - 1, after, pltpu.roll(centre, LANES - 1, 1))
        return centre + coef * (up + down + left + right - 4.0 * centre)

    def column(step, side):
        return jnp.broadcast_to(col_in[step, side], (LANES, rows)).T

    loads[0].wait()
    beside = jnp.where(j > 0, 1, 0) + jnp.where(j < n_col - 1, 1, 0)
    pl.semaphore_wait(barrier, n_row - 1 + beside)

    send_edges(0, adj)

    loads[1].wait()
    loads[2].wait()
    for t in range(tiles):
        at = slice(t * LANES, (t + 1) * LANES)
        coef = DT * kappa[:, at] / (1.0 + late[:, at] * late[:, at])
        late[:, at] = coef
        value = inner_step(adj, coef, t)
        mid[:, at] = value
        field[t * rows : (t + 1) * rows, :] = DT * (adj[:, at] + value)
    loads[3].wait()
    for t in range(tiles):
        at = slice(t * LANES, (t + 1) * LANES)
        early[:, at] = DT * kappa[:, at] / (1.0 + early[:, at] * early[:, at])

    patches = owner_ref.shape[1]
    entries = patch_ref.shape[-1]
    patch = patch_ref[...]
    named = lax.broadcasted_iota(jnp.int32, (patches, entries), 0) == patch
    named = named.astype(jnp.float32).astype(jnp.bfloat16)
    owner = jnp.broadcast_to(owner_ref[...], (16, patches))
    digit = lax.broadcasted_iota(jnp.int32, (16, patches), 0)
    digits = jnp.where(digit == 0, owner // owned, owner % owned).astype(jnp.float32).astype(jnp.bfloat16)
    dest = jnp.dot(digits, named, preferred_element_type=jnp.float32)
    dest = (dest[0:1] * float(owned) + dest[1:2]).astype(jnp.int32)
    to_row = lax.broadcasted_iota(jnp.int32, (patches, entries), 0) == dest
    to_row = to_row.astype(jnp.float32).astype(jnp.bfloat16)
    entry = lax.broadcasted_iota(jnp.int32, (1, entries), 1)
    block = entry // OV
    across = cols // BS
    block_row, block_col = block // across, block % across
    place = (block_col % group) * (high * tiles) + block_row * tiles + block_col // group
    place = index_ref[...] * nblock + place
    from_block = lax.broadcasted_iota(jnp.int32, (nbasis * nblock, entries), 0) == place
    from_block = from_block.astype(jnp.float32).astype(jnp.bfloat16)
    counts[...] = lax.dot_general(
        to_row, from_block, (((1,), (1,)), ((), ())), preferred_element_type=jnp.float32
    ).astype(jnp.bfloat16)

    def add_edges(step, coef, first, last, left, right):
        first(coef[0:1, :] * row_in[step, 0])
        last(coef[rows - 1 : rows, :] * row_in[step, 1])
        left(jnp.where(lane == 0, tile(coef, 0) * column(step, 0), 0.0))
        right(jnp.where(lane == LANES - 1, tile(coef, tiles - 1) * column(step, 1), 0.0))

    def first_mid(delta):
        mid[0:1, :] += delta
        for t in range(tiles):
            field[t * rows : t * rows + 1, :] += DT * tile(delta, t)

    def last_mid(delta):
        mid[rows - 1 : rows, :] += delta
        for t in range(tiles):
            field[(t + 1) * rows - 1 : (t + 1) * rows, :] += DT * tile(delta, t)

    def left_mid(delta):
        mid[:, 0:LANES] += delta
        field[0:rows, :] += DT * delta

    def right_mid(delta):
        mid[:, cols - LANES : cols] += delta
        field[(tiles - 1) * rows : tiles * rows, :] += DT * delta

    receive_edges(0)
    add_edges(0, late, first_mid, last_mid, left_mid, right_mid)
    send_edges(1, mid)

    part = lax.broadcasted_iota(jnp.int32, (high * tiles, LANES), 1) // BS
    for s in range(depth // LANES):
        lines = [
            jnp.concatenate(
                [
                    field[pl.ds(R * BS + s * group + t, tiles, stride=rows), :]
                    for R in range(high)
                ],
                axis=0,
            )
            for t in range(group)
        ]
        for k in range(group):
            out = None
            for t in range(group):
                shift = (t - k) % group * BS
                moved = pltpu.roll(lines[t], shift, 1) if shift else lines[t]
                out = moved if out is None else jnp.where(part == t, moved, out)
            height = high * tiles
            blocks[k * height : (k + 1) * height, s * LANES : (s + 1) * LANES] = out.astype(
                jnp.bfloat16
            )

    loads[4].wait()
    products = jnp.concatenate(
        [
            jnp.dot(blocks[...], basis[q], preferred_element_type=jnp.float32)
            for q in range(nbasis)
        ],
        axis=0,
    )
    upper = products.astype(jnp.bfloat16)
    lower = (products - upper.astype(jnp.float32)).astype(jnp.bfloat16)

    def partial(r):
        mine = counts[pl.ds(pl.multiple_of(r * owned, owned), owned), :]
        return jnp.dot(mine, upper, preferred_element_type=jnp.float32) + jnp.dot(
            mine, lower, preferred_element_type=jnp.float32
        )

    def share(n):
        return pltpu.make_async_remote_copy(
            src_ref=part_out.at[n],
            dst_ref=part_in.at[n],
            send_sem=part_send.at[n],
            recv_sem=part_recv.at[n],
            device_id={"row": partners[n]},
            device_id_type=MESH,
        )

    for n in range(n_row - 1):
        part_out[n] = partial(partners[n])
        share(n).start()
    own = partial(i)

    receive_edges(1)
    for t in range(tiles):
        at = slice(t * LANES, (t + 1) * LANES)
        start_ref[:, at] = inner_step(mid, early[:, at], t)

    def first_start(delta):
        start_ref[0:1, :] += delta

    def last_start(delta):
        start_ref[rows - 1 : rows, :] += delta

    def left_start(delta):
        start_ref[:, 0:LANES] += delta

    def right_start(delta):
        start_ref[:, cols - LANES : cols] += delta

    add_edges(1, early, first_start, last_start, left_start, right_start)

    for n in range(n_row - 1):
        share(n).wait_recv()
        own = own + part_in[n]
    grad_ref[...] = own
    for n in range(n_row - 1):
        share(n).wait_send()
    for step in range(2):
        for side in range(4):

            @pl.when(sides[side][0])
            def _(step=step, side=side):
                halo(step, side).wait_send()


def on_device(
    n_row,
    n_col,
    adj_final,
    kappa,
    elev_early,
    elev_late,
    basis,
    basis_index,
    intersection_patch,
    owner_row,
):
    rows, cols = adj_final.shape
    nbasis, depth, ncoef = basis.shape[2:]
    nblock = rows * cols // depth
    patches = owner_row.shape[1]
    owned = patches // n_row
    anywhere = pl.BlockSpec(memory_space=pl.ANY)
    near = pl.BlockSpec(memory_space=pltpu.VMEM)
    whole = pltpu.VMEM((rows, cols), jnp.float32)
    start, grad = pl.pallas_call(
        functools.partial(kernel, n_row, n_col),
        out_shape=(
            jax.ShapeDtypeStruct((rows, cols), jnp.float32),
            jax.ShapeDtypeStruct((owned, ncoef), jnp.float32),
        ),
        in_specs=[anywhere] * 5 + [near] * 3,
        out_specs=(near, near),
        scratch_shapes=[
            whole,
            whole,
            whole,
            whole,
            pltpu.VMEM((nbasis, depth, ncoef), jnp.bfloat16),
            whole,
            pltpu.VMEM((cols // LANES * rows, LANES), jnp.float32),
            pltpu.VMEM((nblock, depth), jnp.bfloat16),
            pltpu.VMEM((patches, nbasis * nblock), jnp.bfloat16),
            pltpu.VMEM((2, 2, 1, cols), jnp.float32),
            pltpu.VMEM((2, 2, 1, cols), jnp.float32),
            pltpu.VMEM((2, 2, 1, rows), jnp.float32),
            pltpu.VMEM((2, 2, 1, rows), jnp.float32),
            pltpu.VMEM((max(n_row - 1, 1), owned, ncoef), jnp.float32),
            pltpu.VMEM((max(n_row - 1, 1), owned, ncoef), jnp.float32),
            pltpu.SemaphoreType.DMA((5,)),
            pltpu.SemaphoreType.DMA((2, 4)),
            pltpu.SemaphoreType.DMA((2, 4)),
            pltpu.SemaphoreType.DMA((max(n_row - 1, 1),)),
            pltpu.SemaphoreType.DMA((max(n_row - 1, 1),)),
        ],
        compiler_params=pltpu.CompilerParams(
            collective_id=0, has_side_effects=True, vmem_limit_bytes=48 * 2**20
        ),
    )(
        adj_final,
        kappa,
        elev_early,
        elev_late,
        basis[0, 0],
        basis_index[0],
        intersection_patch[0],
        owner_row,
    )
    return (start, grad[None])


def solution(mesh):
    n_row, n_col = mesh.shape["row"], mesh.shape["col"]
    return jax.shard_map(
        functools.partial(on_device, n_row, n_col),
        mesh=mesh,
        in_specs=(
            P(("mem", "row"), "col"),
            P(("mem", "row"), "col"),
            P(("mem", "row"), "col"),
            P(("mem", "row"), "col"),
            P(("mem", "row"), "col", None, None, None),
            P(("mem", "row"), "col", None),
            P(("mem", "row"), "col", None),
            P(("mem", "col"), None),
        ),
        out_specs=(P(("mem", "row"), "col"), P(("mem", "col"), "row", None)),
        check_vma=False,
    )
```

```python
import functools

import jax
import jax.numpy as jnp
from jax import lax
from jax.experimental import pallas as pl
from jax.experimental.pallas import tpu as pltpu
from jax.sharding import PartitionSpec as P

BS = 32
OV = 4
LANES = 128
DT = 0.2
MESH = pl.DeviceIdType.MESH


def kernel(
    n_row,
    n_col,
    adj_hbm,
    kappa_hbm,
    early_hbm,
    late_hbm,
    basis_hbm,
    index_hbm,
    patch_hbm,
    owner_hbm,
    start_ref,
    grad_ref,
    adj,
    kappa,
    early,
    late,
    basis,
    index_ref,
    patch_ref,
    owner_ref,
    mid,
    field,
    blocks,
    counts,
    row_out,
    row_in,
    col_out,
    col_in,
    part_out,
    part_in,
    load_sem,
    halo_send,
    halo_recv,
    part_send,
    part_recv,
):
    rows, cols = adj.shape
    tiles = cols // LANES
    group = LANES // BS
    high = rows // BS
    nblock = blocks.shape[0]
    nbasis, depth, ncoef = basis.shape
    owned = grad_ref.shape[0]
    i = lax.axis_index("row")
    j = lax.axis_index("col")
    sides = (
        (i > 0, {"row": i - 1}),
        (i < n_row - 1, {"row": i + 1}),
        (j > 0, {"col": j - 1}),
        (j < n_col - 1, {"col": j + 1}),
    )
    partners = [lax.rem(i + step, n_row) for step in range(1, n_row)]

    loads = [
        pltpu.make_async_copy(source, target, load_sem.at[n])
        for n, (source, target) in enumerate(
            (
                (adj_hbm, adj),
                (late_hbm, late),
                (kappa_hbm, kappa),
                (index_hbm, index_ref),
                (patch_hbm, patch_ref),
                (owner_hbm, owner_ref),
                (early_hbm, early),
                (basis_hbm, basis),
            )
        )
    ]

    barrier = pltpu.get_barrier_semaphore()
    for partner in partners:
        pl.semaphore_signal(barrier, inc=1, device_id={"row": partner}, device_id_type=MESH)
    for exists, target in sides[2:]:

        @pl.when(exists)
        def _(target=target):
            pl.semaphore_signal(barrier, inc=1, device_id=target, device_id_type=MESH)

    for load in loads:
        load.start()

    def halo(step, side):
        out, into = (row_out, row_in) if side < 2 else (col_out, col_in)
        return pltpu.make_async_remote_copy(
            src_ref=out.at[step, side % 2],
            dst_ref=into.at[step, 1 - side % 2],
            send_sem=halo_send.at[step, side],
            recv_sem=halo_recv.at[step, side ^ 1],
            device_id=sides[side][1],
            device_id_type=MESH,
        )

    def halo_arrival(step, side):
        into = row_in if side < 2 else col_in
        out = row_out if side < 2 else col_out
        return pltpu.make_async_remote_copy(
            src_ref=out.at[step, side % 2],
            dst_ref=into.at[step, side % 2],
            send_sem=halo_send.at[step, side],
            recv_sem=halo_recv.at[step, side],
            device_id=sides[side][1],
            device_id_type=MESH,
        )

    def send_edges(step, ref):
        row_out[step, 0] = ref[0:1, :]
        row_out[step, 1] = ref[rows - 1 : rows, :]
        col_out[step, 0] = ref[:, 0:LANES].T[0:1, :]
        col_out[step, 1] = ref[:, cols - LANES : cols].T[LANES - 1 : LANES, :]
        for side in range(4):

            @pl.when(sides[side][0])
            def _(side=side):
                halo(step, side).start()

    def receive_edges(step):
        for side in range(4):
            into = row_in if side < 2 else col_in

            @pl.when(sides[side][0])
            def _(side=side):
                halo_arrival(step, side).wait_recv()

            @pl.when(jnp.logical_not(sides[side][0]))
            def _(side=side, into=into):
                into[step, side % 2] = jnp.zeros(into.shape[2:], jnp.float32)

    lane = lax.broadcasted_iota(jnp.int32, (rows, LANES), 1)
    line = lax.broadcasted_iota(jnp.int32, (rows, LANES), 0)

    def tile(ref, t):
        return ref[:, t * LANES : (t + 1) * LANES]

    def inner_step(ref, coef, t):
        centre = tile(ref, t)
        up = jnp.where(line == 0, 0.0, pltpu.roll(centre, 1, 0))
        down = jnp.where(line == rows - 1, 0.0, pltpu.roll(centre, rows - 1, 0))
        before = pltpu.roll(tile(ref, t - 1), 1, 1) if t else 0.0
        after = pltpu.roll(tile(ref, t + 1), LANES - 1, 1) if t < tiles - 1 else 0.0
        left = jnp.where(lane == 0, before, pltpu.roll(centre, 1, 1))
        right = jnp.where(lane == LANES - 1, after, pltpu.roll(centre, LANES - 1, 1))
        return centre + coef * (up + down + left + right - 4.0 * centre)

    def column(step, side):
        return jnp.broadcast_to(col_in[step, side], (LANES, rows)).T

    loads[0].wait()
    beside = jnp.where(j > 0, 1, 0) + jnp.where(j < n_col - 1, 1, 0)
    pl.semaphore_wait(barrier, n_row - 1 + beside)

    send_edges(0, adj)

    loads[1].wait()
    loads[2].wait()
    for t in range(tiles):
        at = slice(t * LANES, (t + 1) * LANES)
        coef = DT * kappa[:, at] / (1.0 + late[:, at] * late[:, at])
        late[:, at] = coef
        value = inner_step(adj, coef, t)
        mid[:, at] = value
        field[t * rows : (t + 1) * rows, :] = DT * (adj[:, at] + value)
    loads[6].wait()
    for t in range(tiles):
        at = slice(t * LANES, (t + 1) * LANES)
        early[:, at] = DT * kappa[:, at] / (1.0 + early[:, at] * early[:, at])

    for load in loads[3:6]:
        load.wait()
    patches = owner_ref.shape[1]
    entries = patch_ref.shape[-1]
    patch = patch_ref[...]
    named = lax.broadcasted_iota(jnp.int32, (patches, entries), 0) == patch
    named = named.astype(jnp.float32).astype(jnp.bfloat16)
    owner = jnp.broadcast_to(owner_ref[...], (16, patches))
    digit = lax.broadcasted_iota(jnp.int32, (16, patches), 0)
    digits = jnp.where(digit == 0, owner // owned, owner % owned).astype(jnp.float32).astype(jnp.bfloat16)
    dest = jnp.dot(digits, named, preferred_element_type=jnp.float32)
    dest = (dest[0:1] * float(owned) + dest[1:2]).astype(jnp.int32)
    to_row = lax.broadcasted_iota(jnp.int32, (patches, entries), 0) == dest
    to_row = to_row.astype(jnp.float32).astype(jnp.bfloat16)
    entry = lax.broadcasted_iota(jnp.int32, (1, entries), 1)
    block = entry // OV
    across = cols // BS
    block_row, block_col = block // across, block % across
    place = (block_col % group) * (high * tiles) + block_row * tiles + block_col // group
    place = index_ref[...] * nblock + place
    from_block = lax.broadcasted_iota(jnp.int32, (nbasis * nblock, entries), 0) == place
    from_block = from_block.astype(jnp.float32).astype(jnp.bfloat16)
    counts[...] = lax.dot_general(
        to_row, from_block, (((1,), (1,)), ((), ())), preferred_element_type=jnp.float32
    ).astype(jnp.bfloat16)

    def add_edges(step, coef, first, last, left, right):
        first(coef[0:1, :] * row_in[step, 0])
        last(coef[rows - 1 : rows, :] * row_in[step, 1])
        left(jnp.where(lane == 0, tile(coef, 0) * column(step, 0), 0.0))
        right(jnp.where(lane == LANES - 1, tile(coef, tiles - 1) * column(step, 1), 0.0))

    def first_mid(delta):
        mid[0:1, :] += delta
        for t in range(tiles):
            field[t * rows : t * rows + 1, :] += DT * tile(delta, t)

    def last_mid(delta):
        mid[rows - 1 : rows, :] += delta
        for t in range(tiles):
            field[(t + 1) * rows - 1 : (t + 1) * rows, :] += DT * tile(delta, t)

    def left_mid(delta):
        mid[:, 0:LANES] += delta
        field[0:rows, :] += DT * delta

    def right_mid(delta):
        mid[:, cols - LANES : cols] += delta
        field[(tiles - 1) * rows : tiles * rows, :] += DT * delta

    receive_edges(0)
    add_edges(0, late, first_mid, last_mid, left_mid, right_mid)
    send_edges(1, mid)

    part = lax.broadcasted_iota(jnp.int32, (high * tiles, LANES), 1) // BS
    for s in range(depth // LANES):
        lines = [
            jnp.concatenate(
                [
                    field[pl.ds(R * BS + s * group + t, tiles, stride=rows), :]
                    for R in range(high)
                ],
                axis=0,
            )
            for t in range(group)
        ]
        for k in range(group):
            out = None
            for t in range(group):
                shift = (t - k) % group * BS
                moved = pltpu.roll(lines[t], shift, 1) if shift else lines[t]
                out = moved if out is None else jnp.where(part == t, moved, out)
            height = high * tiles
            blocks[k * height : (k + 1) * height, s * LANES : (s + 1) * LANES] = out.astype(
                jnp.bfloat16
            )

    loads[7].wait()
    products = jnp.concatenate(
        [
            jnp.dot(blocks[...], basis[q], preferred_element_type=jnp.float32)
            for q in range(nbasis)
        ],
        axis=0,
    )
    upper = products.astype(jnp.bfloat16)
    lower = (products - upper.astype(jnp.float32)).astype(jnp.bfloat16)

    def partial(r):
        mine = counts[pl.ds(pl.multiple_of(r * owned, owned), owned), :]
        return jnp.dot(mine, upper, preferred_element_type=jnp.float32) + jnp.dot(
            mine, lower, preferred_element_type=jnp.float32
        )

    def share(n):
        return pltpu.make_async_remote_copy(
            src_ref=part_out.at[n],
            dst_ref=part_in.at[n],
            send_sem=part_send.at[n],
            recv_sem=part_recv.at[n],
            device_id={"row": partners[n]},
            device_id_type=MESH,
        )

    for n in range(n_row - 1):
        part_out[n] = partial(partners[n])
        share(n).start()
    own = partial(i)

    receive_edges(1)
    for t in range(tiles):
        at = slice(t * LANES, (t + 1) * LANES)
        start_ref[:, at] = inner_step(mid, early[:, at], t)

    def first_start(delta):
        start_ref[0:1, :] += delta

    def last_start(delta):
        start_ref[rows - 1 : rows, :] += delta

    def left_start(delta):
        start_ref[:, 0:LANES] += delta

    def right_start(delta):
        start_ref[:, cols - LANES : cols] += delta

    add_edges(1, early, first_start, last_start, left_start, right_start)

    for n in range(n_row - 1):
        share(n).wait_recv()
        own = own + part_in[n]
    grad_ref[...] = own
    for n in range(n_row - 1):
        share(n).wait_send()
    for step in range(2):
        for side in range(4):

            @pl.when(sides[side][0])
            def _(step=step, side=side):
                halo(step, side).wait_send()


def on_device(
    n_row,
    n_col,
    adj_final,
    kappa,
    elev_early,
    elev_late,
    basis,
    basis_index,
    intersection_patch,
    owner_row,
):
    rows, cols = adj_final.shape
    nbasis, depth, ncoef = basis.shape[2:]
    nblock = rows * cols // depth
    patches = owner_row.shape[1]
    owned = patches // n_row
    anywhere = pl.BlockSpec(memory_space=pl.ANY)
    near = pl.BlockSpec(memory_space=pltpu.VMEM)
    whole = pltpu.VMEM((rows, cols), jnp.float32)
    start, grad = pl.pallas_call(
        functools.partial(kernel, n_row, n_col),
        out_shape=(
            jax.ShapeDtypeStruct((rows, cols), jnp.float32),
            jax.ShapeDtypeStruct((owned, ncoef), jnp.float32),
        ),
        in_specs=[anywhere] * 8,
        out_specs=(near, near),
        scratch_shapes=[
            whole,
            whole,
            whole,
            whole,
            pltpu.VMEM((nbasis, depth, ncoef), jnp.bfloat16),
            pltpu.VMEM(basis_index.shape[1:], jnp.int32),
            pltpu.VMEM(intersection_patch.shape[1:], jnp.int32),
            pltpu.VMEM(owner_row.shape, jnp.int32),
            whole,
            pltpu.VMEM((cols // LANES * rows, LANES), jnp.float32),
            pltpu.VMEM((nblock, depth), jnp.bfloat16),
            pltpu.VMEM((patches, nbasis * nblock), jnp.bfloat16),
            pltpu.VMEM((2, 2, 1, cols), jnp.float32),
            pltpu.VMEM((2, 2, 1, cols), jnp.float32),
            pltpu.VMEM((2, 2, 1, rows), jnp.float32),
            pltpu.VMEM((2, 2, 1, rows), jnp.float32),
            pltpu.VMEM((max(n_row - 1, 1), owned, ncoef), jnp.float32),
            pltpu.VMEM((max(n_row - 1, 1), owned, ncoef), jnp.float32),
            pltpu.SemaphoreType.DMA((8,)),
            pltpu.SemaphoreType.DMA((2, 4)),
            pltpu.SemaphoreType.DMA((2, 4)),
            pltpu.SemaphoreType.DMA((max(n_row - 1, 1),)),
            pltpu.SemaphoreType.DMA((max(n_row - 1, 1),)),
        ],
        compiler_params=pltpu.CompilerParams(
            collective_id=0, has_side_effects=True, vmem_limit_bytes=63 * 2**20
        ),
    )(
        adj_final,
        kappa,
        elev_early,
        elev_late,
        basis[0, 0],
        basis_index[0],
        intersection_patch[0],
        owner_row,
    )
    return (start, grad[None])


def solution(mesh):
    n_row, n_col = mesh.shape["row"], mesh.shape["col"]
    return jax.shard_map(
        functools.partial(on_device, n_row, n_col),
        mesh=mesh,
        in_specs=(
            P(("mem", "row"), "col"),
            P(("mem", "row"), "col"),
            P(("mem", "row"), "col"),
            P(("mem", "row"), "col"),
            P(("mem", "row"), "col", None, None, None),
            P(("mem", "row"), "col", None),
            P(("mem", "row"), "col", None),
            P(("mem", "col"), None),
        ),
        out_specs=(P(("mem", "row"), "col"), P(("mem", "col"), "row", None)),
        check_vma=False,
    )
```

```python
import functools

import jax
import jax.numpy as jnp
from jax import lax
from jax.experimental import pallas as pl
from jax.experimental.pallas import tpu as pltpu
from jax.sharding import PartitionSpec as P

BS = 32
OV = 4
LANES = 128
DT = 0.2
MESH = pl.DeviceIdType.MESH


def kernel(
    n_row,
    n_col,
    adj_hbm,
    kappa_hbm,
    early_hbm,
    late_hbm,
    basis_hbm,
    index_hbm,
    patch_hbm,
    owner_hbm,
    start_hbm,
    grad_hbm,
    start_ref,
    grad_ref,
    adj,
    kappa,
    early,
    late,
    basis,
    index_ref,
    patch_ref,
    owner_ref,
    mid,
    field,
    blocks,
    counts,
    row_out,
    row_in,
    col_out,
    col_in,
    part_out,
    part_in,
    load_sem,
    halo_send,
    halo_recv,
    part_send,
    part_recv,
):
    rows, cols = adj.shape
    tiles = cols // LANES
    group = LANES // BS
    high = rows // BS
    nblock = blocks.shape[0]
    nbasis, depth, ncoef = basis.shape
    owned = grad_ref.shape[0]
    i = lax.axis_index("row")
    j = lax.axis_index("col")
    sides = (
        (i > 0, {"row": i - 1}),
        (i < n_row - 1, {"row": i + 1}),
        (j > 0, {"col": j - 1}),
        (j < n_col - 1, {"col": j + 1}),
    )
    partners = [lax.rem(i + step, n_row) for step in range(1, n_row)]

    loads = [
        pltpu.make_async_copy(source, target, load_sem.at[n])
        for n, (source, target) in enumerate(
            (
                (adj_hbm, adj),
                (late_hbm, late),
                (kappa_hbm, kappa),
                (index_hbm, index_ref),
                (patch_hbm, patch_ref),
                (owner_hbm, owner_ref),
                (early_hbm, early),
                (basis_hbm, basis),
            )
        )
    ]

    barrier = pltpu.get_barrier_semaphore()
    for partner in partners:
        pl.semaphore_signal(barrier, inc=1, device_id={"row": partner}, device_id_type=MESH)
    for exists, target in sides[2:]:

        @pl.when(exists)
        def _(target=target):
            pl.semaphore_signal(barrier, inc=1, device_id=target, device_id_type=MESH)

    for load in loads[:6]:
        load.start()

    def halo(step, side):
        out, into = (row_out, row_in) if side < 2 else (col_out, col_in)
        return pltpu.make_async_remote_copy(
            src_ref=out.at[step, side % 2],
            dst_ref=into.at[step, 1 - side % 2],
            send_sem=halo_send.at[step, side],
            recv_sem=halo_recv.at[step, side ^ 1],
            device_id=sides[side][1],
            device_id_type=MESH,
        )

    def halo_arrival(step, side):
        into = row_in if side < 2 else col_in
        out = row_out if side < 2 else col_out
        return pltpu.make_async_remote_copy(
            src_ref=out.at[step, side % 2],
            dst_ref=into.at[step, side % 2],
            send_sem=halo_send.at[step, side],
            recv_sem=halo_recv.at[step, side],
            device_id=sides[side][1],
            device_id_type=MESH,
        )

    def send_edges(step, ref):
        row_out[step, 0] = ref[0:1, :]
        row_out[step, 1] = ref[rows - 1 : rows, :]
        col_out[step, 0] = ref[:, 0:LANES].T[0:1, :]
        col_out[step, 1] = ref[:, cols - LANES : cols].T[LANES - 1 : LANES, :]
        for side in range(4):

            @pl.when(sides[side][0])
            def _(side=side):
                halo(step, side).start()

    def receive_edges(step):
        for side in range(4):
            into = row_in if side < 2 else col_in

            @pl.when(sides[side][0])
            def _(side=side):
                halo_arrival(step, side).wait_recv()

            @pl.when(jnp.logical_not(sides[side][0]))
            def _(side=side, into=into):
                into[step, side % 2] = jnp.zeros(into.shape[2:], jnp.float32)

    lane = lax.broadcasted_iota(jnp.int32, (rows, LANES), 1)
    line = lax.broadcasted_iota(jnp.int32, (rows, LANES), 0)

    def tile(ref, t):
        return ref[:, t * LANES : (t + 1) * LANES]

    def inner_step(ref, coef, t):
        centre = tile(ref, t)
        up = jnp.where(line == 0, 0.0, pltpu.roll(centre, 1, 0))
        down = jnp.where(line == rows - 1, 0.0, pltpu.roll(centre, rows - 1, 0))
        before = pltpu.roll(tile(ref, t - 1), 1, 1) if t else 0.0
        after = pltpu.roll(tile(ref, t + 1), LANES - 1, 1) if t < tiles - 1 else 0.0
        left = jnp.where(lane == 0, before, pltpu.roll(centre, 1, 1))
        right = jnp.where(lane == LANES - 1, after, pltpu.roll(centre, LANES - 1, 1))
        return centre + coef * (up + down + left + right - 4.0 * centre)

    def column(step, side):
        return jnp.broadcast_to(col_in[step, side], (LANES, rows)).T

    loads[0].wait()
    for load in loads[6:]:
        load.start()
    beside = jnp.where(j > 0, 1, 0) + jnp.where(j < n_col - 1, 1, 0)
    pl.semaphore_wait(barrier, n_row - 1 + beside)

    send_edges(0, adj)

    loads[1].wait()
    loads[2].wait()
    for t in range(tiles):
        at = slice(t * LANES, (t + 1) * LANES)
        coef = DT * kappa[:, at] / (1.0 + late[:, at] * late[:, at])
        late[:, at] = coef
        value = inner_step(adj, coef, t)
        mid[:, at] = value
        field[t * rows : (t + 1) * rows, :] = DT * (adj[:, at] + value)
    loads[6].wait()
    for t in range(tiles):
        at = slice(t * LANES, (t + 1) * LANES)
        early[:, at] = DT * kappa[:, at] / (1.0 + early[:, at] * early[:, at])

    for load in loads[3:6]:
        load.wait()
    patches = owner_ref.shape[1]
    entries = patch_ref.shape[-1]
    patch = patch_ref[...]
    named = lax.broadcasted_iota(jnp.int32, (patches, entries), 0) == patch
    named = named.astype(jnp.float32).astype(jnp.bfloat16)
    owner = jnp.broadcast_to(owner_ref[...], (16, patches))
    digit = lax.broadcasted_iota(jnp.int32, (16, patches), 0)
    digits = jnp.where(digit == 0, owner // owned, owner % owned).astype(jnp.float32).astype(jnp.bfloat16)
    dest = jnp.dot(digits, named, preferred_element_type=jnp.float32)
    dest = (dest[0:1] * float(owned) + dest[1:2]).astype(jnp.int32)
    to_row = lax.broadcasted_iota(jnp.int32, (patches, entries), 0) == dest
    to_row = to_row.astype(jnp.float32).astype(jnp.bfloat16)
    entry = lax.broadcasted_iota(jnp.int32, (1, entries), 1)
    block = entry // OV
    across = cols // BS
    block_row, block_col = block // across, block % across
    place = (block_col % group) * (high * tiles) + block_row * tiles + block_col // group
    place = index_ref[...] * nblock + place
    from_block = lax.broadcasted_iota(jnp.int32, (nbasis * nblock, entries), 0) == place
    from_block = from_block.astype(jnp.float32).astype(jnp.bfloat16)
    counts[...] = lax.dot_general(
        to_row, from_block, (((1,), (1,)), ((), ())), preferred_element_type=jnp.float32
    ).astype(jnp.bfloat16)

    def add_edges(step, coef, first, last, left, right):
        first(coef[0:1, :] * row_in[step, 0])
        last(coef[rows - 1 : rows, :] * row_in[step, 1])
        left(jnp.where(lane == 0, tile(coef, 0) * column(step, 0), 0.0))
        right(jnp.where(lane == LANES - 1, tile(coef, tiles - 1) * column(step, 1), 0.0))

    def first_mid(delta):
        mid[0:1, :] += delta
        for t in range(tiles):
            field[t * rows : t * rows + 1, :] += DT * tile(delta, t)

    def last_mid(delta):
        mid[rows - 1 : rows, :] += delta
        for t in range(tiles):
            field[(t + 1) * rows - 1 : (t + 1) * rows, :] += DT * tile(delta, t)

    def left_mid(delta):
        mid[:, 0:LANES] += delta
        field[0:rows, :] += DT * delta

    def right_mid(delta):
        mid[:, cols - LANES : cols] += delta
        field[(tiles - 1) * rows : tiles * rows, :] += DT * delta

    receive_edges(0)
    add_edges(0, late, first_mid, last_mid, left_mid, right_mid)
    send_edges(1, mid)

    part = lax.broadcasted_iota(jnp.int32, (high * tiles, LANES), 1) // BS
    for s in range(depth // LANES):
        lines = [
            jnp.concatenate(
                [
                    field[pl.ds(R * BS + s * group + t, tiles, stride=rows), :]
                    for R in range(high)
                ],
                axis=0,
            )
            for t in range(group)
        ]
        for k in range(group):
            out = None
            for t in range(group):
                shift = (t - k) % group * BS
                moved = pltpu.roll(lines[t], shift, 1) if shift else lines[t]
                out = moved if out is None else jnp.where(part == t, moved, out)
            height = high * tiles
            blocks[k * height : (k + 1) * height, s * LANES : (s + 1) * LANES] = out.astype(
                jnp.bfloat16
            )

    loads[7].wait()
    products = jnp.concatenate(
        [
            jnp.dot(blocks[...], basis[q], preferred_element_type=jnp.float32)
            for q in range(nbasis)
        ],
        axis=0,
    )
    upper = products.astype(jnp.bfloat16)
    lower = (products - upper.astype(jnp.float32)).astype(jnp.bfloat16)

    def partial(r):
        mine = counts[pl.ds(pl.multiple_of(r * owned, owned), owned), :]
        return jnp.dot(mine, upper, preferred_element_type=jnp.float32) + jnp.dot(
            mine, lower, preferred_element_type=jnp.float32
        )

    def share(n):
        return pltpu.make_async_remote_copy(
            src_ref=part_out.at[n],
            dst_ref=part_in.at[n],
            send_sem=part_send.at[n],
            recv_sem=part_recv.at[n],
            device_id={"row": partners[n]},
            device_id_type=MESH,
        )

    for n in range(n_row - 1):
        part_out[n] = partial(partners[n])
        share(n).start()
    own = partial(i)

    receive_edges(1)
    for t in range(tiles):
        at = slice(t * LANES, (t + 1) * LANES)
        start_ref[:, at] = inner_step(mid, early[:, at], t)

    def first_start(delta):
        start_ref[0:1, :] += delta

    def last_start(delta):
        start_ref[rows - 1 : rows, :] += delta

    def left_start(delta):
        start_ref[:, 0:LANES] += delta

    def right_start(delta):
        start_ref[:, cols - LANES : cols] += delta

    add_edges(1, early, first_start, last_start, left_start, right_start)
    stores = [
        pltpu.make_async_copy(start_ref, start_hbm, load_sem.at[8]),
        pltpu.make_async_copy(grad_ref, grad_hbm, load_sem.at[9]),
    ]
    stores[0].start()

    for n in range(n_row - 1):
        share(n).wait_recv()
        own = own + part_in[n]
    grad_ref[...] = own
    stores[1].start()
    for n in range(n_row - 1):
        share(n).wait_send()
    for step in range(2):
        for side in range(4):

            @pl.when(sides[side][0])
            def _(step=step, side=side):
                halo(step, side).wait_send()

    for store in stores:
        store.wait()


def place_results(start_from, grad_from, start_to, grad_to, sem):
    quarter = start_from.shape[0] // 4
    copies = [
        pltpu.make_async_copy(
            start_from.at[pl.ds(n * quarter, quarter)],
            start_to.at[pl.ds(n * quarter, quarter)],
            sem.at[n],
        )
        for n in range(4)
    ] + [pltpu.make_async_copy(grad_from, grad_to, sem.at[4])]
    for copy in copies:
        copy.start()
    for copy in copies:
        copy.wait()


def on_device(
    n_row,
    n_col,
    adj_final,
    kappa,
    elev_early,
    elev_late,
    basis,
    basis_index,
    intersection_patch,
    owner_row,
):
    rows, cols = adj_final.shape
    nbasis, depth, ncoef = basis.shape[2:]
    nblock = rows * cols // depth
    patches = owner_row.shape[1]
    owned = patches // n_row
    far = pl.BlockSpec(memory_space=pl.ANY)
    whole = pltpu.VMEM((rows, cols), jnp.float32)
    start, grad = pl.pallas_call(
        functools.partial(kernel, n_row, n_col),
        out_shape=(
            jax.ShapeDtypeStruct((rows, cols), jnp.float32),
            jax.ShapeDtypeStruct((owned, ncoef), jnp.float32),
        ),
        in_specs=[far] * 8,
        out_specs=(far, far),
        scratch_shapes=[
            whole,
            pltpu.VMEM((owned, ncoef), jnp.float32),
            whole,
            whole,
            whole,
            whole,
            pltpu.VMEM((nbasis, depth, ncoef), jnp.bfloat16),
            pltpu.VMEM(basis_index.shape[1:], jnp.int32),
            pltpu.VMEM(intersection_patch.shape[1:], jnp.int32),
            pltpu.VMEM(owner_row.shape, jnp.int32),
            whole,
            pltpu.VMEM((cols // LANES * rows, LANES), jnp.float32),
            pltpu.VMEM((nblock, depth), jnp.bfloat16),
            pltpu.VMEM((patches, nbasis * nblock), jnp.bfloat16),
            pltpu.VMEM((2, 2, 1, cols), jnp.float32),
            pltpu.VMEM((2, 2, 1, cols), jnp.float32),
            pltpu.VMEM((2, 2, 1, rows), jnp.float32),
            pltpu.VMEM((2, 2, 1, rows), jnp.float32),
            pltpu.VMEM((max(n_row - 1, 1), owned, ncoef), jnp.float32),
            pltpu.VMEM((max(n_row - 1, 1), owned, ncoef), jnp.float32),
            pltpu.SemaphoreType.DMA((10,)),
            pltpu.SemaphoreType.DMA((2, 4)),
            pltpu.SemaphoreType.DMA((2, 4)),
            pltpu.SemaphoreType.DMA((max(n_row - 1, 1),)),
            pltpu.SemaphoreType.DMA((max(n_row - 1, 1),)),
        ],
        compiler_params=pltpu.CompilerParams(
            collective_id=0, has_side_effects=True, vmem_limit_bytes=63 * 2**20
        ),
    )(
        adj_final,
        kappa,
        elev_early,
        elev_late,
        basis[0, 0],
        basis_index[0],
        intersection_patch[0],
        owner_row,
    )
    start, grad = pl.pallas_call(
        place_results,
        out_shape=(
            jax.ShapeDtypeStruct(start.shape, jnp.float32),
            jax.ShapeDtypeStruct(grad.shape, jnp.float32),
        ),
        in_specs=[far, far],
        out_specs=(far, far),
        scratch_shapes=[pltpu.SemaphoreType.DMA((5,))],
        compiler_params=pltpu.CompilerParams(vmem_limit_bytes=63 * 2**20),
    )(start, grad)
    return (start, grad[None])


def solution(mesh):
    n_row, n_col = mesh.shape["row"], mesh.shape["col"]
    return jax.shard_map(
        functools.partial(on_device, n_row, n_col),
        mesh=mesh,
        in_specs=(
            P(("mem", "row"), "col"),
            P(("mem", "row"), "col"),
            P(("mem", "row"), "col"),
            P(("mem", "row"), "col"),
            P(("mem", "row"), "col", None, None, None),
            P(("mem", "row"), "col", None),
            P(("mem", "row"), "col", None),
            P(("mem", "col"), None),
        ),
        out_specs=(P(("mem", "row"), "col"), P(("mem", "col"), "row", None)),
        check_vma=False,
    )
```

```python
import functools

import jax
import jax.numpy as jnp
from jax import lax
from jax.experimental import pallas as pl
from jax.experimental.pallas import tpu as pltpu
from jax.sharding import PartitionSpec as P

BS = 32
OV = 4
LANES = 128
DT = 0.2
MESH = pl.DeviceIdType.MESH


def kernel(
    n_row,
    n_col,
    adj_hbm,
    kappa_hbm,
    early_hbm,
    late_hbm,
    basis_hbm,
    index_hbm,
    patch_hbm,
    owner_hbm,
    start_hbm,
    grad_hbm,
    start_ref,
    grad_ref,
    adj,
    kappa,
    early,
    late,
    basis,
    index_ref,
    patch_ref,
    owner_ref,
    mid,
    field,
    blocks,
    counts,
    row_out,
    row_in,
    col_out,
    col_in,
    part_out,
    part_in,
    load_sem,
    halo_send,
    halo_recv,
    part_send,
    part_recv,
):
    rows, cols = adj.shape
    tiles = cols // LANES
    group = LANES // BS
    high = rows // BS
    nblock = blocks.shape[0]
    nbasis, depth, ncoef = basis.shape
    owned = grad_ref.shape[0]
    i = lax.axis_index("row")
    j = lax.axis_index("col")
    sides = (
        (i > 0, {"row": i - 1}),
        (i < n_row - 1, {"row": i + 1}),
        (j > 0, {"col": j - 1}),
        (j < n_col - 1, {"col": j + 1}),
    )
    partners = [lax.rem(i + step, n_row) for step in range(1, n_row)]

    loads = [
        pltpu.make_async_copy(source, target, load_sem.at[n])
        for n, (source, target) in enumerate(
            (
                (adj_hbm, adj),
                (late_hbm, late),
                (kappa_hbm, kappa),
                (index_hbm, index_ref),
                (patch_hbm, patch_ref),
                (owner_hbm, owner_ref),
                (early_hbm, early),
                (basis_hbm, basis),
            )
        )
    ]

    barrier = pltpu.get_barrier_semaphore()
    for partner in partners:
        pl.semaphore_signal(barrier, inc=1, device_id={"row": partner}, device_id_type=MESH)
    for exists, target in sides[2:]:

        @pl.when(exists)
        def _(target=target):
            pl.semaphore_signal(barrier, inc=1, device_id=target, device_id_type=MESH)

    for load in loads[:6]:
        load.start()

    def halo(step, side):
        out, into = (row_out, row_in) if side < 2 else (col_out, col_in)
        return pltpu.make_async_remote_copy(
            src_ref=out.at[step, side % 2],
            dst_ref=into.at[step, 1 - side % 2],
            send_sem=halo_send.at[step, side],
            recv_sem=halo_recv.at[step, side ^ 1],
            device_id=sides[side][1],
            device_id_type=MESH,
        )

    def halo_arrival(step, side):
        into = row_in if side < 2 else col_in
        out = row_out if side < 2 else col_out
        return pltpu.make_async_remote_copy(
            src_ref=out.at[step, side % 2],
            dst_ref=into.at[step, side % 2],
            send_sem=halo_send.at[step, side],
            recv_sem=halo_recv.at[step, side],
            device_id=sides[side][1],
            device_id_type=MESH,
        )

    def send_edges(step, ref):
        row_out[step, 0] = ref[0:1, :]
        row_out[step, 1] = ref[rows - 1 : rows, :]
        col_out[step, 0] = ref[:, 0:LANES].T[0:1, :]
        col_out[step, 1] = ref[:, cols - LANES : cols].T[LANES - 1 : LANES, :]
        for side in range(4):

            @pl.when(sides[side][0])
            def _(side=side):
                halo(step, side).start()

    def receive_edges(step):
        for side in range(4):
            into = row_in if side < 2 else col_in

            @pl.when(sides[side][0])
            def _(side=side):
                halo_arrival(step, side).wait_recv()

            @pl.when(jnp.logical_not(sides[side][0]))
            def _(side=side, into=into):
                into[step, side % 2] = jnp.zeros(into.shape[2:], jnp.float32)

    lane = lax.broadcasted_iota(jnp.int32, (rows, LANES), 1)
    line = lax.broadcasted_iota(jnp.int32, (rows, LANES), 0)

    def tile(ref, t):
        return ref[:, t * LANES : (t + 1) * LANES]

    def inner_step(ref, coef, t):
        centre = tile(ref, t)
        up = jnp.where(line == 0, 0.0, pltpu.roll(centre, 1, 0))
        down = jnp.where(line == rows - 1, 0.0, pltpu.roll(centre, rows - 1, 0))
        before = pltpu.roll(tile(ref, t - 1), 1, 1) if t else 0.0
        after = pltpu.roll(tile(ref, t + 1), LANES - 1, 1) if t < tiles - 1 else 0.0
        left = jnp.where(lane == 0, before, pltpu.roll(centre, 1, 1))
        right = jnp.where(lane == LANES - 1, after, pltpu.roll(centre, LANES - 1, 1))
        return centre + coef * (up + down + left + right - 4.0 * centre)

    def column(step, side):
        return jnp.broadcast_to(col_in[step, side], (LANES, rows)).T

    loads[0].wait()
    for load in loads[6:]:
        load.start()
    beside = jnp.where(j > 0, 1, 0) + jnp.where(j < n_col - 1, 1, 0)
    pl.semaphore_wait(barrier, n_row - 1 + beside)

    send_edges(0, adj)

    loads[1].wait()
    loads[2].wait()
    for t in range(tiles):
        at = slice(t * LANES, (t + 1) * LANES)
        coef = DT * kappa[:, at] / (1.0 + late[:, at] * late[:, at])
        late[:, at] = coef
        value = inner_step(adj, coef, t)
        mid[:, at] = value
        field[t * rows : (t + 1) * rows, :] = DT * (adj[:, at] + value)
    loads[6].wait()
    for t in range(tiles):
        at = slice(t * LANES, (t + 1) * LANES)
        early[:, at] = DT * kappa[:, at] / (1.0 + early[:, at] * early[:, at])

    for load in loads[3:6]:
        load.wait()
    patches = owner_ref.shape[1]
    entries = patch_ref.shape[-1]
    patch = patch_ref[...]
    named = lax.broadcasted_iota(jnp.int32, (patches, entries), 0) == patch
    named = named.astype(jnp.float32).astype(jnp.bfloat16)
    owner = jnp.broadcast_to(owner_ref[...], (16, patches))
    digit = lax.broadcasted_iota(jnp.int32, (16, patches), 0)
    digits = jnp.where(digit == 0, owner // owned, owner % owned).astype(jnp.float32).astype(jnp.bfloat16)
    dest = jnp.dot(digits, named, preferred_element_type=jnp.float32)
    dest = (dest[0:1] * float(owned) + dest[1:2]).astype(jnp.int32)
    to_row = lax.broadcasted_iota(jnp.int32, (patches, entries), 0) == dest
    to_row = to_row.astype(jnp.float32).astype(jnp.bfloat16)
    entry = lax.broadcasted_iota(jnp.int32, (1, entries), 1)
    block = entry // OV
    across = cols // BS
    block_row, block_col = block // across, block % across
    place = (block_col % group) * (high * tiles) + block_row * tiles + block_col // group
    place = index_ref[...] * nblock + place
    from_block = lax.broadcasted_iota(jnp.int32, (nbasis * nblock, entries), 0) == place
    from_block = from_block.astype(jnp.float32).astype(jnp.bfloat16)
    counts[...] = lax.dot_general(
        to_row, from_block, (((1,), (1,)), ((), ())), preferred_element_type=jnp.float32
    ).astype(jnp.bfloat16)

    def add_edges(step, coef, first, last, left, right):
        first(coef[0:1, :] * row_in[step, 0])
        last(coef[rows - 1 : rows, :] * row_in[step, 1])
        left(jnp.where(lane == 0, tile(coef, 0) * column(step, 0), 0.0))
        right(jnp.where(lane == LANES - 1, tile(coef, tiles - 1) * column(step, 1), 0.0))

    def first_mid(delta):
        mid[0:1, :] += delta
        for t in range(tiles):
            field[t * rows : t * rows + 1, :] += DT * tile(delta, t)

    def last_mid(delta):
        mid[rows - 1 : rows, :] += delta
        for t in range(tiles):
            field[(t + 1) * rows - 1 : (t + 1) * rows, :] += DT * tile(delta, t)

    def left_mid(delta):
        mid[:, 0:LANES] += delta
        field[0:rows, :] += DT * delta

    def right_mid(delta):
        mid[:, cols - LANES : cols] += delta
        field[(tiles - 1) * rows : tiles * rows, :] += DT * delta

    receive_edges(0)
    add_edges(0, late, first_mid, last_mid, left_mid, right_mid)
    send_edges(1, mid)

    part = lax.broadcasted_iota(jnp.int32, (high * tiles, LANES), 1) // BS
    for s in range(depth // LANES):
        lines = [
            jnp.concatenate(
                [
                    field[pl.ds(R * BS + s * group + t, tiles, stride=rows), :]
                    for R in range(high)
                ],
                axis=0,
            )
            for t in range(group)
        ]
        for k in range(group):
            out = None
            for t in range(group):
                shift = (t - k) % group * BS
                moved = pltpu.roll(lines[t], shift, 1) if shift else lines[t]
                out = moved if out is None else jnp.where(part == t, moved, out)
            height = high * tiles
            blocks[k * height : (k + 1) * height, s * LANES : (s + 1) * LANES] = out.astype(
                jnp.bfloat16
            )

    loads[7].wait()
    products = jnp.concatenate(
        [
            jnp.dot(blocks[...], basis[q], preferred_element_type=jnp.float32)
            for q in range(nbasis)
        ],
        axis=0,
    )
    upper = products.astype(jnp.bfloat16)
    lower = (products - upper.astype(jnp.float32)).astype(jnp.bfloat16)

    def partial(r):
        mine = counts[pl.ds(pl.multiple_of(r * owned, owned), owned), :]
        return jnp.dot(mine, upper, preferred_element_type=jnp.float32) + jnp.dot(
            mine, lower, preferred_element_type=jnp.float32
        )

    def share(n):
        return pltpu.make_async_remote_copy(
            src_ref=part_out.at[n],
            dst_ref=part_in.at[n],
            send_sem=part_send.at[n],
            recv_sem=part_recv.at[n],
            device_id={"row": partners[n]},
            device_id_type=MESH,
        )

    for n in range(n_row - 1):
        part_out[n] = partial(partners[n])
        share(n).start()
    own = partial(i)

    receive_edges(1)
    for t in range(tiles):
        at = slice(t * LANES, (t + 1) * LANES)
        start_ref[:, at] = inner_step(mid, early[:, at], t)

    def first_start(delta):
        start_ref[0:1, :] += delta

    def last_start(delta):
        start_ref[rows - 1 : rows, :] += delta

    def left_start(delta):
        start_ref[:, 0:LANES] += delta

    def right_start(delta):
        start_ref[:, cols - LANES : cols] += delta

    add_edges(1, early, first_start, last_start, left_start, right_start)
    stores = [
        pltpu.make_async_copy(start_ref, start_hbm, load_sem.at[8]),
        pltpu.make_async_copy(grad_ref, grad_hbm, load_sem.at[9]),
    ]
    stores[0].start()

    for n in range(n_row - 1):
        share(n).wait_recv()
        own = own + part_in[n]
    grad_ref[...] = own
    stores[1].start()
    for n in range(n_row - 1):
        share(n).wait_send()
    for step in range(2):
        for side in range(4):

            @pl.when(sides[side][0])
            def _(step=step, side=side):
                halo(step, side).wait_send()

    for store in stores:
        store.wait()


def place_results(start_from, grad_from, start_to, grad_to, start, grad, load_sem, store_sem):
    half = start.shape[0] // 2
    pieces = [
        (start_from.at[pl.ds(n * half, half)], start.at[pl.ds(n * half, half)], start_to.at[pl.ds(n * half, half)])
        for n in range(2)
    ] + [(grad_from, grad, grad_to)]
    loads = [
        pltpu.make_async_copy(source, held, load_sem.at[n])
        for n, (source, held, _) in enumerate(pieces)
    ]
    stores = [
        pltpu.make_async_copy(held, target, store_sem.at[n])
        for n, (_, held, target) in enumerate(pieces)
    ]
    for load in loads:
        load.start()
    for load, store in zip(loads, stores):
        load.wait()
        store.start()
    for store in stores:
        store.wait()


def on_device(
    n_row,
    n_col,
    adj_final,
    kappa,
    elev_early,
    elev_late,
    basis,
    basis_index,
    intersection_patch,
    owner_row,
):
    rows, cols = adj_final.shape
    nbasis, depth, ncoef = basis.shape[2:]
    nblock = rows * cols // depth
    patches = owner_row.shape[1]
    owned = patches // n_row
    far = pl.BlockSpec(memory_space=pl.ANY)
    whole = pltpu.VMEM((rows, cols), jnp.float32)
    start, grad = pl.pallas_call(
        functools.partial(kernel, n_row, n_col),
        out_shape=(
            jax.ShapeDtypeStruct((rows, cols), jnp.float32),
            jax.ShapeDtypeStruct((owned, ncoef), jnp.float32),
        ),
        in_specs=[far] * 8,
        out_specs=(far, far),
        scratch_shapes=[
            whole,
            pltpu.VMEM((owned, ncoef), jnp.float32),
            whole,
            whole,
            whole,
            whole,
            pltpu.VMEM((nbasis, depth, ncoef), jnp.bfloat16),
            pltpu.VMEM(basis_index.shape[1:], jnp.int32),
            pltpu.VMEM(intersection_patch.shape[1:], jnp.int32),
            pltpu.VMEM(owner_row.shape, jnp.int32),
            whole,
            pltpu.VMEM((cols // LANES * rows, LANES), jnp.float32),
            pltpu.VMEM((nblock, depth), jnp.bfloat16),
            pltpu.VMEM((patches, nbasis * nblock), jnp.bfloat16),
            pltpu.VMEM((2, 2, 1, cols), jnp.float32),
            pltpu.VMEM((2, 2, 1, cols), jnp.float32),
            pltpu.VMEM((2, 2, 1, rows), jnp.float32),
            pltpu.VMEM((2, 2, 1, rows), jnp.float32),
            pltpu.VMEM((max(n_row - 1, 1), owned, ncoef), jnp.float32),
            pltpu.VMEM((max(n_row - 1, 1), owned, ncoef), jnp.float32),
            pltpu.SemaphoreType.DMA((10,)),
            pltpu.SemaphoreType.DMA((2, 4)),
            pltpu.SemaphoreType.DMA((2, 4)),
            pltpu.SemaphoreType.DMA((max(n_row - 1, 1),)),
            pltpu.SemaphoreType.DMA((max(n_row - 1, 1),)),
        ],
        compiler_params=pltpu.CompilerParams(
            collective_id=0, has_side_effects=True, vmem_limit_bytes=63 * 2**20
        ),
    )(
        adj_final,
        kappa,
        elev_early,
        elev_late,
        basis[0, 0],
        basis_index[0],
        intersection_patch[0],
        owner_row,
    )
    start, grad = pl.pallas_call(
        place_results,
        out_shape=(
            jax.ShapeDtypeStruct(start.shape, jnp.float32),
            jax.ShapeDtypeStruct(grad.shape, jnp.float32),
        ),
        in_specs=[far, far],
        out_specs=(far, far),
        scratch_shapes=[
            whole,
            pltpu.VMEM((owned, ncoef), jnp.float32),
            pltpu.SemaphoreType.DMA((3,)),
            pltpu.SemaphoreType.DMA((3,)),
        ],
        compiler_params=pltpu.CompilerParams(vmem_limit_bytes=63 * 2**20),
    )(start, grad)
    return (start, grad[None])


def solution(mesh):
    n_row, n_col = mesh.shape["row"], mesh.shape["col"]
    return jax.shard_map(
        functools.partial(on_device, n_row, n_col),
        mesh=mesh,
        in_specs=(
            P(("mem", "row"), "col"),
            P(("mem", "row"), "col"),
            P(("mem", "row"), "col"),
            P(("mem", "row"), "col"),
            P(("mem", "row"), "col", None, None, None),
            P(("mem", "row"), "col", None),
            P(("mem", "row"), "col", None),
            P(("mem", "col"), None),
        ),
        out_specs=(P(("mem", "row"), "col"), P(("mem", "col"), "row", None)),
        check_vma=False,
    )
```

```python
import functools

import jax
import jax.numpy as jnp
from jax import lax
from jax.experimental import pallas as pl
from jax.experimental.pallas import tpu as pltpu
from jax.sharding import PartitionSpec as P

BS = 32
OV = 4
LANES = 128
DT = 0.2
MESH = pl.DeviceIdType.MESH


def kernel(
    n_row,
    n_col,
    adj_hbm,
    kappa_hbm,
    early_hbm,
    late_hbm,
    basis_hbm,
    index_hbm,
    patch_hbm,
    owner_hbm,
    start_hbm,
    grad_hbm,
    start_ref,
    grad_ref,
    adj,
    kappa,
    early,
    late,
    basis,
    index_ref,
    patch_ref,
    owner_ref,
    mid,
    field,
    blocks,
    counts,
    row_out,
    row_in,
    col_out,
    col_in,
    part_out,
    part_in,
    load_sem,
    halo_send,
    halo_recv,
    part_send,
    part_recv,
):
    rows, cols = adj.shape
    tiles = cols // LANES
    group = LANES // BS
    high = rows // BS
    nblock = blocks.shape[0]
    nbasis, depth, ncoef = basis.shape
    owned = grad_ref.shape[0]
    i = lax.axis_index("row")
    j = lax.axis_index("col")
    sides = (
        (i > 0, {"row": i - 1}),
        (i < n_row - 1, {"row": i + 1}),
        (j > 0, {"col": j - 1}),
        (j < n_col - 1, {"col": j + 1}),
    )
    partners = [lax.rem(i + step, n_row) for step in range(1, n_row)]

    loads = [
        pltpu.make_async_copy(source, target, load_sem.at[n])
        for n, (source, target) in enumerate(
            (
                (adj_hbm, adj),
                (late_hbm, late),
                (kappa_hbm, kappa),
                (index_hbm, index_ref),
                (patch_hbm, patch_ref),
                (owner_hbm, owner_ref),
                (early_hbm, early),
                (basis_hbm, basis),
            )
        )
    ]

    barrier = pltpu.get_barrier_semaphore()
    for partner in partners:
        pl.semaphore_signal(barrier, inc=1, device_id={"row": partner}, device_id_type=MESH)
    for exists, target in sides[2:]:

        @pl.when(exists)
        def _(target=target):
            pl.semaphore_signal(barrier, inc=1, device_id=target, device_id_type=MESH)

    for load in loads[:6]:
        load.start()

    def halo(step, side):
        out, into = (row_out, row_in) if side < 2 else (col_out, col_in)
        return pltpu.make_async_remote_copy(
            src_ref=out.at[step, side % 2],
            dst_ref=into.at[step, 1 - side % 2],
            send_sem=halo_send.at[step, side],
            recv_sem=halo_recv.at[step, side ^ 1],
            device_id=sides[side][1],
            device_id_type=MESH,
        )

    def halo_arrival(step, side):
        into = row_in if side < 2 else col_in
        out = row_out if side < 2 else col_out
        return pltpu.make_async_remote_copy(
            src_ref=out.at[step, side % 2],
            dst_ref=into.at[step, side % 2],
            send_sem=halo_send.at[step, side],
            recv_sem=halo_recv.at[step, side],
            device_id=sides[side][1],
            device_id_type=MESH,
        )

    def send_edges(step, ref):
        row_out[step, 0] = ref[0:1, :]
        row_out[step, 1] = ref[rows - 1 : rows, :]
        col_out[step, 0] = ref[:, 0:LANES].T[0:1, :]
        col_out[step, 1] = ref[:, cols - LANES : cols].T[LANES - 1 : LANES, :]
        for side in range(4):

            @pl.when(sides[side][0])
            def _(side=side):
                halo(step, side).start()

    def receive_edges(step):
        for side in range(4):
            into = row_in if side < 2 else col_in

            @pl.when(sides[side][0])
            def _(side=side):
                halo_arrival(step, side).wait_recv()

            @pl.when(jnp.logical_not(sides[side][0]))
            def _(side=side, into=into):
                into[step, side % 2] = jnp.zeros(into.shape[2:], jnp.float32)

    lane = lax.broadcasted_iota(jnp.int32, (rows, LANES), 1)
    line = lax.broadcasted_iota(jnp.int32, (rows, LANES), 0)

    def tile(ref, t):
        return ref[:, t * LANES : (t + 1) * LANES]

    def inner_step(ref, coef, t):
        centre = tile(ref, t)
        up = jnp.where(line == 0, 0.0, pltpu.roll(centre, 1, 0))
        down = jnp.where(line == rows - 1, 0.0, pltpu.roll(centre, rows - 1, 0))
        before = pltpu.roll(tile(ref, t - 1), 1, 1) if t else 0.0
        after = pltpu.roll(tile(ref, t + 1), LANES - 1, 1) if t < tiles - 1 else 0.0
        left = jnp.where(lane == 0, before, pltpu.roll(centre, 1, 1))
        right = jnp.where(lane == LANES - 1, after, pltpu.roll(centre, LANES - 1, 1))
        return centre + coef * (up + down + left + right - 4.0 * centre)

    def column(step, side):
        return jnp.broadcast_to(col_in[step, side], (LANES, rows)).T

    loads[0].wait()
    for load in loads[6:]:
        load.start()
    beside = jnp.where(j > 0, 1, 0) + jnp.where(j < n_col - 1, 1, 0)
    pl.semaphore_wait(barrier, n_row - 1 + beside)

    send_edges(0, adj)

    loads[1].wait()
    loads[2].wait()
    for t in range(tiles):
        at = slice(t * LANES, (t + 1) * LANES)
        coef = DT * kappa[:, at] / (1.0 + late[:, at] * late[:, at])
        late[:, at] = coef
        value = inner_step(adj, coef, t)
        mid[:, at] = value
        field[t * rows : (t + 1) * rows, :] = DT * (adj[:, at] + value)
    loads[6].wait()
    for t in range(tiles):
        at = slice(t * LANES, (t + 1) * LANES)
        early[:, at] = DT * kappa[:, at] / (1.0 + early[:, at] * early[:, at])

    for load in loads[3:6]:
        load.wait()
    patches = owner_ref.shape[1]
    entries = patch_ref.shape[-1]
    patch = patch_ref[...]
    named = lax.broadcasted_iota(jnp.int32, (patches, entries), 0) == patch
    named = named.astype(jnp.float32).astype(jnp.bfloat16)
    owner = jnp.broadcast_to(owner_ref[...], (16, patches))
    digit = lax.broadcasted_iota(jnp.int32, (16, patches), 0)
    digits = jnp.where(digit == 0, owner // owned, owner % owned).astype(jnp.float32).astype(jnp.bfloat16)
    dest = jnp.dot(digits, named, preferred_element_type=jnp.float32)
    dest = (dest[0:1] * float(owned) + dest[1:2]).astype(jnp.int32)
    to_row = lax.broadcasted_iota(jnp.int32, (patches, entries), 0) == dest
    to_row = to_row.astype(jnp.float32).astype(jnp.bfloat16)
    entry = lax.broadcasted_iota(jnp.int32, (1, entries), 1)
    block = entry // OV
    across = cols // BS
    block_row, block_col = block // across, block % across
    place = (block_col % group) * (high * tiles) + block_row * tiles + block_col // group
    place = index_ref[...] * nblock + place
    from_block = lax.broadcasted_iota(jnp.int32, (nbasis * nblock, entries), 0) == place
    from_block = from_block.astype(jnp.float32).astype(jnp.bfloat16)
    counts[...] = lax.dot_general(
        to_row, from_block, (((1,), (1,)), ((), ())), preferred_element_type=jnp.float32
    ).astype(jnp.bfloat16)

    def add_edges(step, coef, first, last, left, right):
        first(coef[0:1, :] * row_in[step, 0])
        last(coef[rows - 1 : rows, :] * row_in[step, 1])
        left(jnp.where(lane == 0, tile(coef, 0) * column(step, 0), 0.0))
        right(jnp.where(lane == LANES - 1, tile(coef, tiles - 1) * column(step, 1), 0.0))

    def first_mid(delta):
        mid[0:1, :] += delta
        for t in range(tiles):
            field[t * rows : t * rows + 1, :] += DT * tile(delta, t)

    def last_mid(delta):
        mid[rows - 1 : rows, :] += delta
        for t in range(tiles):
            field[(t + 1) * rows - 1 : (t + 1) * rows, :] += DT * tile(delta, t)

    def left_mid(delta):
        mid[:, 0:LANES] += delta
        field[0:rows, :] += DT * delta

    def right_mid(delta):
        mid[:, cols - LANES : cols] += delta
        field[(tiles - 1) * rows : tiles * rows, :] += DT * delta

    receive_edges(0)
    add_edges(0, late, first_mid, last_mid, left_mid, right_mid)
    send_edges(1, mid)

    part = lax.broadcasted_iota(jnp.int32, (high * tiles, LANES), 1) // BS
    for s in range(depth // LANES):
        lines = [
            jnp.concatenate(
                [
                    field[pl.ds(R * BS + s * group + t, tiles, stride=rows), :]
                    for R in range(high)
                ],
                axis=0,
            )
            for t in range(group)
        ]
        for k in range(group):
            out = None
            for t in range(group):
                shift = (t - k) % group * BS
                moved = pltpu.roll(lines[t], shift, 1) if shift else lines[t]
                out = moved if out is None else jnp.where(part == t, moved, out)
            height = high * tiles
            blocks[k * height : (k + 1) * height, s * LANES : (s + 1) * LANES] = out.astype(
                jnp.bfloat16
            )

    loads[7].wait()
    products = jnp.concatenate(
        [
            jnp.dot(blocks[...], basis[q], preferred_element_type=jnp.float32)
            for q in range(nbasis)
        ],
        axis=0,
    )
    upper = products.astype(jnp.bfloat16)
    lower = (products - upper.astype(jnp.float32)).astype(jnp.bfloat16)

    def partial(r):
        mine = counts[pl.ds(pl.multiple_of(r * owned, owned), owned), :]
        return jnp.dot(mine, upper, preferred_element_type=jnp.float32) + jnp.dot(
            mine, lower, preferred_element_type=jnp.float32
        )

    def share(n):
        return pltpu.make_async_remote_copy(
            src_ref=part_out.at[n],
            dst_ref=part_in.at[n],
            send_sem=part_send.at[n],
            recv_sem=part_recv.at[n],
            device_id={"row": partners[n]},
            device_id_type=MESH,
        )

    for n in range(n_row - 1):
        part_out[n] = partial(partners[n])
        share(n).start()
    own = partial(i)

    for t in range(tiles):
        at = slice(t * LANES, (t + 1) * LANES)
        start_ref[:, at] = inner_step(mid, early[:, at], t)

    def first_start(delta):
        start_ref[0:1, :] += delta

    def last_start(delta):
        start_ref[rows - 1 : rows, :] += delta

    def left_start(delta):
        start_ref[:, 0:LANES] += delta

    def right_start(delta):
        start_ref[:, cols - LANES : cols] += delta

    receive_edges(1)
    add_edges(1, early, first_start, last_start, left_start, right_start)
    stores = [
        pltpu.make_async_copy(start_ref, start_hbm, load_sem.at[8]),
        pltpu.make_async_copy(grad_ref, grad_hbm, load_sem.at[9]),
    ]
    stores[0].start()

    for n in range(n_row - 1):
        share(n).wait_recv()
        own = own + part_in[n]
    grad_ref[...] = own
    stores[1].start()
    for n in range(n_row - 1):
        share(n).wait_send()
    for step in range(2):
        for side in range(4):

            @pl.when(sides[side][0])
            def _(step=step, side=side):
                halo(step, side).wait_send()

    for store in stores:
        store.wait()


def place_results(start_from, grad_from, start_to, grad_to, start, grad, load_sem, store_sem):
    half = start.shape[0] // 2
    pieces = [
        (start_from.at[pl.ds(n * half, half)], start.at[pl.ds(n * half, half)], start_to.at[pl.ds(n * half, half)])
        for n in range(2)
    ] + [(grad_from, grad, grad_to)]
    loads = [
        pltpu.make_async_copy(source, held, load_sem.at[n])
        for n, (source, held, _) in enumerate(pieces)
    ]
    stores = [
        pltpu.make_async_copy(held, target, store_sem.at[n])
        for n, (_, held, target) in enumerate(pieces)
    ]
    for load in loads:
        load.start()
    for load, store in zip(loads, stores):
        load.wait()
        store.start()
    for store in stores:
        store.wait()


def on_device(
    n_row,
    n_col,
    adj_final,
    kappa,
    elev_early,
    elev_late,
    basis,
    basis_index,
    intersection_patch,
    owner_row,
):
    rows, cols = adj_final.shape
    nbasis, depth, ncoef = basis.shape[2:]
    nblock = rows * cols // depth
    patches = owner_row.shape[1]
    owned = patches // n_row
    far = pl.BlockSpec(memory_space=pl.ANY)
    whole = pltpu.VMEM((rows, cols), jnp.float32)
    start, grad = pl.pallas_call(
        functools.partial(kernel, n_row, n_col),
        out_shape=(
            jax.ShapeDtypeStruct((rows, cols), jnp.float32),
            jax.ShapeDtypeStruct((owned, ncoef), jnp.float32),
        ),
        in_specs=[far] * 8,
        out_specs=(far, far),
        scratch_shapes=[
            whole,
            pltpu.VMEM((owned, ncoef), jnp.float32),
            whole,
            whole,
            whole,
            whole,
            pltpu.VMEM((nbasis, depth, ncoef), jnp.bfloat16),
            pltpu.VMEM(basis_index.shape[1:], jnp.int32),
            pltpu.VMEM(intersection_patch.shape[1:], jnp.int32),
            pltpu.VMEM(owner_row.shape, jnp.int32),
            whole,
            pltpu.VMEM((cols // LANES * rows, LANES), jnp.float32),
            pltpu.VMEM((nblock, depth), jnp.bfloat16),
            pltpu.VMEM((patches, nbasis * nblock), jnp.bfloat16),
            pltpu.VMEM((2, 2, 1, cols), jnp.float32),
            pltpu.VMEM((2, 2, 1, cols), jnp.float32),
            pltpu.VMEM((2, 2, 1, rows), jnp.float32),
            pltpu.VMEM((2, 2, 1, rows), jnp.float32),
            pltpu.VMEM((max(n_row - 1, 1), owned, ncoef), jnp.float32),
            pltpu.VMEM((max(n_row - 1, 1), owned, ncoef), jnp.float32),
            pltpu.SemaphoreType.DMA((10,)),
            pltpu.SemaphoreType.DMA((2, 4)),
            pltpu.SemaphoreType.DMA((2, 4)),
            pltpu.SemaphoreType.DMA((max(n_row - 1, 1),)),
            pltpu.SemaphoreType.DMA((max(n_row - 1, 1),)),
        ],
        compiler_params=pltpu.CompilerParams(
            collective_id=0, has_side_effects=True, vmem_limit_bytes=63 * 2**20
        ),
    )(
        adj_final,
        kappa,
        elev_early,
        elev_late,
        basis[0, 0],
        basis_index[0],
        intersection_patch[0],
        owner_row,
    )
    start, grad = pl.pallas_call(
        place_results,
        out_shape=(
            jax.ShapeDtypeStruct(start.shape, jnp.float32),
            jax.ShapeDtypeStruct(grad.shape, jnp.float32),
        ),
        in_specs=[far, far],
        out_specs=(far, far),
        scratch_shapes=[
            whole,
            pltpu.VMEM((owned, ncoef), jnp.float32),
            pltpu.SemaphoreType.DMA((3,)),
            pltpu.SemaphoreType.DMA((3,)),
        ],
        compiler_params=pltpu.CompilerParams(vmem_limit_bytes=63 * 2**20),
    )(start, grad)
    return (start, grad[None])


def solution(mesh):
    n_row, n_col = mesh.shape["row"], mesh.shape["col"]
    return jax.shard_map(
        functools.partial(on_device, n_row, n_col),
        mesh=mesh,
        in_specs=(
            P(("mem", "row"), "col"),
            P(("mem", "row"), "col"),
            P(("mem", "row"), "col"),
            P(("mem", "row"), "col"),
            P(("mem", "row"), "col", None, None, None),
            P(("mem", "row"), "col", None),
            P(("mem", "row"), "col", None),
            P(("mem", "col"), None),
        ),
        out_specs=(P(("mem", "row"), "col"), P(("mem", "col"), "row", None)),
        check_vma=False,
    )
```

```python
import functools

import jax
import jax.numpy as jnp
from jax import lax
from jax.experimental import pallas as pl
from jax.experimental.pallas import tpu as pltpu
from jax.sharding import PartitionSpec as P

BS = 32
OV = 4
LANES = 128
DT = 0.2
MESH = pl.DeviceIdType.MESH


def kernel(
    n_row,
    n_col,
    adj_hbm,
    kappa_hbm,
    early_hbm,
    late_hbm,
    basis_hbm,
    index_hbm,
    patch_hbm,
    owner_hbm,
    start_hbm,
    grad_hbm,
    start_ref,
    grad_ref,
    adj,
    kappa,
    early,
    late,
    basis,
    index_ref,
    patch_ref,
    owner_ref,
    mid,
    field,
    blocks,
    counts,
    row_out,
    row_in,
    col_out,
    col_in,
    part_out,
    part_in,
    load_sem,
    halo_send,
    halo_recv,
    part_send,
    part_recv,
):
    rows, cols = adj.shape
    tiles = cols // LANES
    group = LANES // BS
    high = rows // BS
    nblock = blocks.shape[0]
    nbasis, depth, ncoef = basis.shape
    owned = grad_ref.shape[0]
    i = lax.axis_index("row")
    j = lax.axis_index("col")
    sides = (
        (i > 0, {"row": i - 1}),
        (i < n_row - 1, {"row": i + 1}),
        (j > 0, {"col": j - 1}),
        (j < n_col - 1, {"col": j + 1}),
    )
    partners = [lax.rem(i + step, n_row) for step in range(1, n_row)]

    loads = [
        pltpu.make_async_copy(source, target, load_sem.at[n])
        for n, (source, target) in enumerate(
            (
                (adj_hbm, adj),
                (late_hbm, late),
                (kappa_hbm, kappa),
                (index_hbm, index_ref),
                (patch_hbm, patch_ref),
                (owner_hbm, owner_ref),
                (early_hbm, early),
                (basis_hbm, basis),
            )
        )
    ]

    barrier = pltpu.get_barrier_semaphore()
    for partner in partners:
        pl.semaphore_signal(barrier, inc=1, device_id={"row": partner}, device_id_type=MESH)
    for exists, target in sides[2:]:

        @pl.when(exists)
        def _(target=target):
            pl.semaphore_signal(barrier, inc=1, device_id=target, device_id_type=MESH)

    quarter = rows // 4
    first = [
        pltpu.make_async_copy(
            adj_hbm.at[pl.ds(n * quarter, quarter)],
            adj.at[pl.ds(n * quarter, quarter)],
            load_sem.at[10 + n],
        )
        for n in range(4)
    ]
    for load in first + loads[1:6]:
        load.start()

    def halo(step, side):
        out, into = (row_out, row_in) if side < 2 else (col_out, col_in)
        return pltpu.make_async_remote_copy(
            src_ref=out.at[step, side % 2],
            dst_ref=into.at[step, 1 - side % 2],
            send_sem=halo_send.at[step, side],
            recv_sem=halo_recv.at[step, side ^ 1],
            device_id=sides[side][1],
            device_id_type=MESH,
        )

    def halo_arrival(step, side):
        into = row_in if side < 2 else col_in
        out = row_out if side < 2 else col_out
        return pltpu.make_async_remote_copy(
            src_ref=out.at[step, side % 2],
            dst_ref=into.at[step, side % 2],
            send_sem=halo_send.at[step, side],
            recv_sem=halo_recv.at[step, side],
            device_id=sides[side][1],
            device_id_type=MESH,
        )

    def send_edges(step, ref):
        row_out[step, 0] = ref[0:1, :]
        row_out[step, 1] = ref[rows - 1 : rows, :]
        col_out[step, 0] = ref[:, 0:LANES].T[0:1, :]
        col_out[step, 1] = ref[:, cols - LANES : cols].T[LANES - 1 : LANES, :]
        for side in range(4):

            @pl.when(sides[side][0])
            def _(side=side):
                halo(step, side).start()

    def receive_edges(step):
        for side in range(4):
            into = row_in if side < 2 else col_in

            @pl.when(sides[side][0])
            def _(side=side):
                halo_arrival(step, side).wait_recv()

            @pl.when(jnp.logical_not(sides[side][0]))
            def _(side=side, into=into):
                into[step, side % 2] = jnp.zeros(into.shape[2:], jnp.float32)

    lane = lax.broadcasted_iota(jnp.int32, (rows, LANES), 1)
    line = lax.broadcasted_iota(jnp.int32, (rows, LANES), 0)

    def tile(ref, t):
        return ref[:, t * LANES : (t + 1) * LANES]

    def inner_step(ref, coef, t):
        centre = tile(ref, t)
        up = jnp.where(line == 0, 0.0, pltpu.roll(centre, 1, 0))
        down = jnp.where(line == rows - 1, 0.0, pltpu.roll(centre, rows - 1, 0))
        before = pltpu.roll(tile(ref, t - 1), 1, 1) if t else 0.0
        after = pltpu.roll(tile(ref, t + 1), LANES - 1, 1) if t < tiles - 1 else 0.0
        left = jnp.where(lane == 0, before, pltpu.roll(centre, 1, 1))
        right = jnp.where(lane == LANES - 1, after, pltpu.roll(centre, LANES - 1, 1))
        return centre + coef * (up + down + left + right - 4.0 * centre)

    def column(step, side):
        return jnp.broadcast_to(col_in[step, side], (LANES, rows)).T

    for load in first:
        load.wait()
    for load in loads[6:]:
        load.start()
    beside = jnp.where(j > 0, 1, 0) + jnp.where(j < n_col - 1, 1, 0)
    pl.semaphore_wait(barrier, n_row - 1 + beside)

    send_edges(0, adj)

    loads[1].wait()
    loads[2].wait()
    for t in range(tiles):
        at = slice(t * LANES, (t + 1) * LANES)
        coef = DT * kappa[:, at] / (1.0 + late[:, at] * late[:, at])
        late[:, at] = coef
        value = inner_step(adj, coef, t)
        mid[:, at] = value
        field[t * rows : (t + 1) * rows, :] = DT * (adj[:, at] + value)
    loads[6].wait()
    for t in range(tiles):
        at = slice(t * LANES, (t + 1) * LANES)
        early[:, at] = DT * kappa[:, at] / (1.0 + early[:, at] * early[:, at])

    for load in loads[3:6]:
        load.wait()
    patches = owner_ref.shape[1]
    entries = patch_ref.shape[-1]
    patch = patch_ref[...]
    named = lax.broadcasted_iota(jnp.int32, (patches, entries), 0) == patch
    named = named.astype(jnp.float32).astype(jnp.bfloat16)
    owner = jnp.broadcast_to(owner_ref[...], (16, patches))
    digit = lax.broadcasted_iota(jnp.int32, (16, patches), 0)
    digits = jnp.where(digit == 0, owner // owned, owner % owned).astype(jnp.float32).astype(jnp.bfloat16)
    dest = jnp.dot(digits, named, preferred_element_type=jnp.float32)
    dest = (dest[0:1] * float(owned) + dest[1:2]).astype(jnp.int32)
    to_row = lax.broadcasted_iota(jnp.int32, (patches, entries), 0) == dest
    to_row = to_row.astype(jnp.float32).astype(jnp.bfloat16)
    entry = lax.broadcasted_iota(jnp.int32, (1, entries), 1)
    block = entry // OV
    across = cols // BS
    block_row, block_col = block // across, block % across
    place = (block_col % group) * (high * tiles) + block_row * tiles + block_col // group
    place = index_ref[...] * nblock + place
    from_block = lax.broadcasted_iota(jnp.int32, (nbasis * nblock, entries), 0) == place
    from_block = from_block.astype(jnp.float32).astype(jnp.bfloat16)
    counts[...] = lax.dot_general(
        to_row, from_block, (((1,), (1,)), ((), ())), preferred_element_type=jnp.float32
    ).astype(jnp.bfloat16)

    def add_edges(step, coef, first, last, left, right):
        first(coef[0:1, :] * row_in[step, 0])
        last(coef[rows - 1 : rows, :] * row_in[step, 1])
        left(jnp.where(lane == 0, tile(coef, 0) * column(step, 0), 0.0))
        right(jnp.where(lane == LANES - 1, tile(coef, tiles - 1) * column(step, 1), 0.0))

    def first_mid(delta):
        mid[0:1, :] += delta
        for t in range(tiles):
            field[t * rows : t * rows + 1, :] += DT * tile(delta, t)

    def last_mid(delta):
        mid[rows - 1 : rows, :] += delta
        for t in range(tiles):
            field[(t + 1) * rows - 1 : (t + 1) * rows, :] += DT * tile(delta, t)

    def left_mid(delta):
        mid[:, 0:LANES] += delta
        field[0:rows, :] += DT * delta

    def right_mid(delta):
        mid[:, cols - LANES : cols] += delta
        field[(tiles - 1) * rows : tiles * rows, :] += DT * delta

    receive_edges(0)
    add_edges(0, late, first_mid, last_mid, left_mid, right_mid)
    send_edges(1, mid)

    part = lax.broadcasted_iota(jnp.int32, (high * tiles, LANES), 1) // BS
    for s in range(depth // LANES):
        lines = [
            jnp.concatenate(
                [
                    field[pl.ds(R * BS + s * group + t, tiles, stride=rows), :]
                    for R in range(high)
                ],
                axis=0,
            )
            for t in range(group)
        ]
        for k in range(group):
            out = None
            for t in range(group):
                shift = (t - k) % group * BS
                moved = pltpu.roll(lines[t], shift, 1) if shift else lines[t]
                out = moved if out is None else jnp.where(part == t, moved, out)
            height = high * tiles
            blocks[k * height : (k + 1) * height, s * LANES : (s + 1) * LANES] = out.astype(
                jnp.bfloat16
            )

    loads[7].wait()
    products = jnp.concatenate(
        [
            jnp.dot(blocks[...], basis[q], preferred_element_type=jnp.float32)
            for q in range(nbasis)
        ],
        axis=0,
    )
    upper = products.astype(jnp.bfloat16)
    lower = (products - upper.astype(jnp.float32)).astype(jnp.bfloat16)

    def partial(r):
        mine = counts[pl.ds(pl.multiple_of(r * owned, owned), owned), :]
        return jnp.dot(mine, upper, preferred_element_type=jnp.float32) + jnp.dot(
            mine, lower, preferred_element_type=jnp.float32
        )

    def share(n):
        return pltpu.make_async_remote_copy(
            src_ref=part_out.at[n],
            dst_ref=part_in.at[n],
            send_sem=part_send.at[n],
            recv_sem=part_recv.at[n],
            device_id={"row": partners[n]},
            device_id_type=MESH,
        )

    for n in range(n_row - 1):
        part_out[n] = partial(partners[n])
        share(n).start()
    own = partial(i)

    receive_edges(1)
    for t in range(tiles):
        at = slice(t * LANES, (t + 1) * LANES)
        start_ref[:, at] = inner_step(mid, early[:, at], t)

    def first_start(delta):
        start_ref[0:1, :] += delta

    def last_start(delta):
        start_ref[rows - 1 : rows, :] += delta

    def left_start(delta):
        start_ref[:, 0:LANES] += delta

    def right_start(delta):
        start_ref[:, cols - LANES : cols] += delta

    add_edges(1, early, first_start, last_start, left_start, right_start)
    stores = [
        pltpu.make_async_copy(start_ref, start_hbm, load_sem.at[8]),
        pltpu.make_async_copy(grad_ref, grad_hbm, load_sem.at[9]),
    ]
    stores[0].start()

    for n in range(n_row - 1):
        share(n).wait_recv()
        own = own + part_in[n]
    grad_ref[...] = own
    stores[1].start()
    for n in range(n_row - 1):
        share(n).wait_send()
    for step in range(2):
        for side in range(4):

            @pl.when(sides[side][0])
            def _(step=step, side=side):
                halo(step, side).wait_send()

    for store in stores:
        store.wait()


def place_results(start_from, grad_from, start_to, grad_to, start, grad, load_sem, store_sem):
    piece = start.shape[0] // 4
    pieces = [
        (start_from.at[pl.ds(n * piece, piece)], start.at[pl.ds(n * piece, piece)], start_to.at[pl.ds(n * piece, piece)])
        for n in range(4)
    ] + [(grad_from, grad, grad_to)]
    loads = [
        pltpu.make_async_copy(source, held, load_sem.at[n])
        for n, (source, held, _) in enumerate(pieces)
    ]
    stores = [
        pltpu.make_async_copy(held, target, store_sem.at[n])
        for n, (_, held, target) in enumerate(pieces)
    ]
    for load in loads:
        load.start()
    for load, store in zip(loads, stores):
        load.wait()
        store.start()
    for store in stores:
        store.wait()


def on_device(
    n_row,
    n_col,
    adj_final,
    kappa,
    elev_early,
    elev_late,
    basis,
    basis_index,
    intersection_patch,
    owner_row,
):
    rows, cols = adj_final.shape
    nbasis, depth, ncoef = basis.shape[2:]
    nblock = rows * cols // depth
    patches = owner_row.shape[1]
    owned = patches // n_row
    far = pl.BlockSpec(memory_space=pl.ANY)
    whole = pltpu.VMEM((rows, cols), jnp.float32)
    start, grad = pl.pallas_call(
        functools.partial(kernel, n_row, n_col),
        out_shape=(
            jax.ShapeDtypeStruct((rows, cols), jnp.float32),
            jax.ShapeDtypeStruct((owned, ncoef), jnp.float32),
        ),
        in_specs=[far] * 8,
        out_specs=(far, far),
        scratch_shapes=[
            whole,
            pltpu.VMEM((owned, ncoef), jnp.float32),
            whole,
            whole,
            whole,
            whole,
            pltpu.VMEM((nbasis, depth, ncoef), jnp.bfloat16),
            pltpu.VMEM(basis_index.shape[1:], jnp.int32),
            pltpu.VMEM(intersection_patch.shape[1:], jnp.int32),
            pltpu.VMEM(owner_row.shape, jnp.int32),
            whole,
            pltpu.VMEM((cols // LANES * rows, LANES), jnp.float32),
            pltpu.VMEM((nblock, depth), jnp.bfloat16),
            pltpu.VMEM((patches, nbasis * nblock), jnp.bfloat16),
            pltpu.VMEM((2, 2, 1, cols), jnp.float32),
            pltpu.VMEM((2, 2, 1, cols), jnp.float32),
            pltpu.VMEM((2, 2, 1, rows), jnp.float32),
            pltpu.VMEM((2, 2, 1, rows), jnp.float32),
            pltpu.VMEM((max(n_row - 1, 1), owned, ncoef), jnp.float32),
            pltpu.VMEM((max(n_row - 1, 1), owned, ncoef), jnp.float32),
            pltpu.SemaphoreType.DMA((14,)),
            pltpu.SemaphoreType.DMA((2, 4)),
            pltpu.SemaphoreType.DMA((2, 4)),
            pltpu.SemaphoreType.DMA((max(n_row - 1, 1),)),
            pltpu.SemaphoreType.DMA((max(n_row - 1, 1),)),
        ],
        compiler_params=pltpu.CompilerParams(
            collective_id=0, has_side_effects=True, vmem_limit_bytes=63 * 2**20
        ),
    )(
        adj_final,
        kappa,
        elev_early,
        elev_late,
        basis[0, 0],
        basis_index[0],
        intersection_patch[0],
        owner_row,
    )
    start, grad = pl.pallas_call(
        place_results,
        out_shape=(
            jax.ShapeDtypeStruct(start.shape, jnp.float32),
            jax.ShapeDtypeStruct(grad.shape, jnp.float32),
        ),
        in_specs=[far, far],
        out_specs=(far, far),
        scratch_shapes=[
            whole,
            pltpu.VMEM((owned, ncoef), jnp.float32),
            pltpu.SemaphoreType.DMA((5,)),
            pltpu.SemaphoreType.DMA((5,)),
        ],
        compiler_params=pltpu.CompilerParams(vmem_limit_bytes=63 * 2**20),
    )(start, grad)
    return (start, grad[None])


def solution(mesh):
    n_row, n_col = mesh.shape["row"], mesh.shape["col"]
    return jax.shard_map(
        functools.partial(on_device, n_row, n_col),
        mesh=mesh,
        in_specs=(
            P(("mem", "row"), "col"),
            P(("mem", "row"), "col"),
            P(("mem", "row"), "col"),
            P(("mem", "row"), "col"),
            P(("mem", "row"), "col", None, None, None),
            P(("mem", "row"), "col", None),
            P(("mem", "row"), "col", None),
            P(("mem", "col"), None),
        ),
        out_specs=(P(("mem", "row"), "col"), P(("mem", "col"), "row", None)),
        check_vma=False,
    )
```
